32 devices in a mesh: space: 8 (over z, x), chan: 4 (over y, core).
Axes of the slice: x: 2, y: 2, z: 4, core: 2. Of those that a mesh axis runs over, the one named last changes fastest.
Arguments:
- volume: bfloat16 [16, 256, 8, 128], P('space', 'chan'), may hold values from -6 to 6
- kernel: bfloat16 [27, 256, 256], P(None, 'chan'), may hold values from -0.078125 to 0.078125
- cotangent: bfloat16 [16, 256, 8, 128], P('space', 'chan'), may hold values from -6 to 6
Outputs:
- output_map: bfloat16 [16, 256, 8, 128], P('space', 'chan')
- input_grad: bfloat16 [16, 256, 8, 128], P('space', 'chan')
- kernel_grad: float32 [27, 256, 256], P(None, 'chan')
The draws below stay inside these ranges and needn't reach their ends.
All inputs are finite; a program needn't handle non-finite values.
Results may differ from the reference program's by a relative error of at most 0.001.
Values may be sent and summed in bfloat16 or wider, within the bound.
No kernel may reach another device: no remote copies, remote signals or barrier semaphores. Data moves between devices by JAX's collectives and lax.ppermute only.
A program may use at most 128 MiB of HBM per device.

```python
import math
import jax
import jax.numpy as jnp
from jax import lax

C = 256
F = 256
H = 8
W = 128
NZ = 16


def shard_levels(stream_key, extent, shards, low, high):
    gain, own = 1.0, jax.random.fold_in(stream_key, 6)
    for axis_at, parts in shards:
        steps = jnp.exp(jax.random.uniform(jax.random.fold_in(own, axis_at), (parts,), jnp.float32, low / len(shards), high / len(shards)))
        gain = gain * jnp.repeat(steps, extent[axis_at] // parts).reshape([-1 if axis == axis_at else 1 for axis in range(len(extent))])
    return gain


def centred(own_key, dims, deviation, bound, split=(), kind=jnp.bfloat16):
    gain = shard_levels(own_key, dims, split, -0.22, 0.18) if split else 1.0
    drawn = jax.random.normal(own_key, dims, jnp.float32) * deviation * gain
    return jnp.minimum(jnp.maximum(drawn, -bound), bound).astype(kind)


def setup_inputs(seed: int = 0) -> dict:
    splits = jax.random.split(jax.random.key(seed), 4)
    volume = centred(splits[0], (NZ, C, H, W), 1.0, 6.0, ((0, 8), (1, 4)))
    kernel = centred(splits[1], (27, F, C), (27 * C) ** -0.5, 0.078125, ((1, 4),))
    cotangent = centred(splits[2], (NZ, F, H, W), 1.0, 6.0, ((0, 8), (1, 4)))
    return dict(volume=volume, kernel=kernel, cotangent=cotangent)


def pad_cells(block):
    return jnp.pad(block, ((1, 1), (0, 0), (1, 1), (1, 1)))

def reference(volume, kernel, cotangent):
    volume_full = volume.astype(jnp.float32)
    grad_full = cotangent.astype(jnp.float32)
    kernel_full = kernel.astype(jnp.float32)
    volume_pad = pad_cells(volume_full)
    grad_pad = pad_cells(grad_full)
    output_sum = jnp.zeros((NZ, F, H, W), jnp.float32)
    input_sum = jnp.zeros((NZ, C, H, W), jnp.float32)
    kernel_terms = []
    for tap_index in range(27):
        depth_step = tap_index // 9
        row_step = tap_index // 3 % 3
        col_step = tap_index % 3
        window = volume_pad[depth_step:depth_step + NZ, :, row_step:row_step + H, col_step:col_step + W]
        output_sum = output_sum + jnp.einsum('fc,zchw->zfhw', kernel_full[tap_index], window, precision=lax.Precision.HIGHEST)
        kernel_terms.append(jnp.einsum('zfhw,zchw->fc', grad_full, window, precision=lax.Precision.HIGHEST))
        back_window = grad_pad[2 - depth_step:2 - depth_step + NZ, :, 2 - row_step:2 - row_step + H, 2 - col_step:2 - col_step + W]
        input_sum = input_sum + jnp.einsum('fc,zfhw->zchw', kernel_full[tap_index], back_window, precision=lax.Precision.HIGHEST)
    scale_factor = 1.0 / math.sqrt(NZ * H * W)
    kernel_grad = jnp.stack(kernel_terms) * scale_factor
    return (output_sum.astype(jnp.bfloat16), input_sum.astype(jnp.bfloat16), kernel_grad)
```

```python
import functools
import math

import jax
import jax.numpy as jnp
from jax import lax
from jax.experimental import pallas as pl
from jax.experimental.pallas import tpu as pltpu
from jax.sharding import PartitionSpec as P

VMEM_LIMIT = 48 * 1024 * 1024


def vmem_specs(count):
    return [pl.BlockSpec(memory_space=pltpu.VMEM)] * count


def shifted(block, step, width):
    if step == 0:
        return block
    lane = lax.broadcasted_iota(jnp.int32, block.shape, 1)
    rolled = pltpu.roll(block.astype(jnp.float32), (-step) % width, 1)
    kept = (lane + step >= 0) & (lane + step < width)
    return jnp.where(kept, rolled, 0.0).astype(block.dtype)


def kernel_grad_kernel(
    scale, order, place, own, other, grad, grad_low, grad_high, out_ref, bound_ref, left, right
):
    depth, height, chans, width = own.shape
    filters = grad.shape[2]
    cells = height * width
    span = 2 * chans

    def grad_row(plane, row):
        if plane == 0:
            return grad_low[row]
        if plane == depth + 1:
            return grad_high[row]
        return grad[plane - 1, row]

    for source, at in ((own, place[0]), (other, 1 - place[0])):
        for plane in range(depth):
            for row in range(height):
                lanes = slice(plane * cells + row * width, plane * cells + (row + 1) * width)
                block = source[plane, row]
                for col_step in range(3):
                    start = pl.multiple_of(col_step * span + at * chans, chans)
                    right[pl.ds(start, chans), lanes] = shifted(block, col_step - 1, width)
    for a in range(3):
        for b in range(3):
            rows = slice((3 * a + b) * filters, (3 * a + b + 1) * filters)
            for plane in range(depth):
                for row in range(height):
                    lanes = slice(plane * cells + row * width, plane * cells + (row + 1) * width)
                    at = row - b + 1
                    if 0 <= at < height:
                        left[rows, lanes] = grad_row(plane - a + 2, at)
                    else:
                        left[rows, lanes] = jnp.zeros((filters, width), left.dtype)
    total = lax.dot_general(
        left[...], right[...], (((1,), (1,)), ((), ())), preferred_element_type=jnp.float32
    )
    total = total * scale
    peak = jnp.maximum(jnp.max(jnp.abs(total)), 1e-30)
    bound_ref[...] = jnp.ceil(jnp.log2(jnp.full(bound_ref.shape, peak, jnp.float32))) + 1.0
    rows = out_ref.shape[1]
    for tap in range(27):
        a, b, c = tap // 9, tap // 3 % 3, tap % 3
        block = total[(3 * a + b) * filters : (3 * a + b + 1) * filters, c * span : (c + 1) * span]
        for shard, at in enumerate(order):
            out_ref[at * 27 + tap] = block[shard * rows : (shard + 1) * rows]


def kernel_grad_part(place, own, other, grad, grad_low, grad_high, scale, order):
    depth, height, chans, width = own.shape
    filters = grad.shape[2]
    cells = depth * height * width
    rows = filters // len(order)
    return pl.pallas_call(
        functools.partial(kernel_grad_kernel, scale, order),
        out_shape=[
            jax.ShapeDtypeStruct((27 * len(order), rows, 2 * chans), jnp.float32),
            jax.ShapeDtypeStruct((rows, 2 * chans), jnp.float32),
        ],
        in_specs=[pl.BlockSpec(memory_space=pltpu.SMEM)] + vmem_specs(5),
        out_specs=vmem_specs(2),
        scratch_shapes=[
            pltpu.VMEM((9 * filters, cells), jnp.bfloat16),
            pltpu.VMEM((6 * chans, cells), jnp.bfloat16),
        ],
        compiler_params=pltpu.CompilerParams(vmem_limit_bytes=VMEM_LIMIT),
        cost_estimate=pl.CostEstimate(
            flops=2 * 27 * filters * 2 * chans * cells, bytes_accessed=4 << 20, transcendentals=0
        ),
        name="kernel_grad",
    )(place, own, other, grad, grad_low, grad_high)


def output_kernel(place, own, other, far_own, far_other, rims, taps, out_ref, weights, stack, acc):
    depth, height, chans, width = own.shape
    filters, total = taps.shape[1], taps.shape[2]
    cells = height * width
    for tap in range(27):
        a, b, c = tap // 9, tap // 3 % 3, tap % 3
        weights[(3 * a + b) * filters : (3 * a + b + 1) * filters, c * total : (c + 1) * total] = taps[tap]
    core, row_of = place[0], place[1]
    parts = (
        (own, 2 * row_of + core),
        (other, 2 * row_of + 1 - core),
        (far_own, 2 * (1 - row_of) + core),
        (far_other, 2 * (1 - row_of) + 1 - core),
    )
    acc[...] = jnp.zeros_like(acc)
    for plane in range(depth + 2):
        inner = 0 < plane < depth + 1
        for row in range(height):
            lanes = slice(row * width, (row + 1) * width)
            if inner:
                for source, at in parts:
                    block = source[plane - 1, row]
                    for c in range(3):
                        start = pl.multiple_of(c * total + at * chans, chans)
                        stack[pl.ds(start, chans), lanes] = shifted(block, c - 1, width)
            else:
                block = rims[min(plane, 1), row]
                for c in range(3):
                    stack[c * total : (c + 1) * total, lanes] = shifted(block, c - 1, width)
        steps = [a for a in range(3) if 0 <= plane - a < depth]
        low, high = steps[0], steps[-1] + 1
        for row in range(0, height, 2):
            part = jnp.dot(
                weights[low * 3 * filters : high * 3 * filters, :],
                stack[:, row * width : (row + 2) * width],
                preferred_element_type=jnp.float32,
            )
            for a in steps:
                for b in range(3):
                    block = part[((a - low) * 3 + b) * filters : ((a - low) * 3 + b + 1) * filters]
                    for k in range(2):
                        at = row + k - b + 1
                        if 0 <= at < height:
                            acc[plane - a, at] += block[:, k * width : (k + 1) * width]
    out_ref[...] = acc[...].astype(out_ref.dtype)


def output_part(place, own, other, far_own, far_other, rims, taps):
    depth, height, chans, width = own.shape
    filters, total = taps.shape[1], taps.shape[2]
    return pl.pallas_call(
        output_kernel,
        out_shape=jax.ShapeDtypeStruct((depth, height, filters, width), jnp.bfloat16),
        in_specs=[pl.BlockSpec(memory_space=pltpu.SMEM)] + vmem_specs(6),
        out_specs=pl.BlockSpec(memory_space=pltpu.VMEM),
        scratch_shapes=[
            pltpu.VMEM((9 * filters, 3 * total), jnp.bfloat16),
            pltpu.VMEM((3 * total, height * width), jnp.bfloat16),
            pltpu.VMEM((depth, height, filters, width), jnp.float32),
        ],
        compiler_params=pltpu.CompilerParams(vmem_limit_bytes=VMEM_LIMIT),
        cost_estimate=pl.CostEstimate(
            flops=2 * 27 * filters * total * depth * height * width, bytes_accessed=4 << 20, transcendentals=0
        ),
        name="output_map",
    )(place, own, other, far_own, far_other, rims, taps)


def input_grad_kernel(grad, grad_low, grad_high, taps, out_ref, weights, stack):
    depth, height, filters, width = grad.shape
    total = taps.shape[2]
    span = 3 * filters
    weights[...] = jnp.transpose(taps[...].reshape(27 * filters, total))
    zero = jnp.zeros((span, width), stack.dtype)
    for plane in range(depth + 2):
        stack[plane, 0] = zero
        stack[plane, height + 1] = zero
        for row in range(height):
            if plane == 0:
                block = grad_low[row]
            elif plane == depth + 1:
                block = grad_high[row]
            else:
                block = grad[plane - 1, row]
            for c in range(3):
                stack[plane, row + 1, c * filters : (c + 1) * filters] = shifted(block, 1 - c, width)
    chans = out_ref.shape[4]
    for plane in range(depth):
        for row in range(0, height, 2):
            halves = []
            for k in range(2):
                pieces = [stack[plane - a + 2, row + k - b + 2] for a in range(3) for b in range(3)]
                halves.append(jnp.concatenate(pieces, axis=0))
            part = jnp.dot(weights[...], jnp.concatenate(halves, axis=1), preferred_element_type=jnp.float32)
            for k in range(2):
                for block in range(total // chans):
                    out_ref[block // 2, block % 2, plane, row + k] = part[
                        block * chans : (block + 1) * chans, k * width : (k + 1) * width
                    ]


def input_grad_part(grad, grad_low, grad_high, taps, chans):
    depth, height, filters, width = grad.shape
    total = taps.shape[2]
    return pl.pallas_call(
        input_grad_kernel,
        out_shape=jax.ShapeDtypeStruct((2, 2, depth, height, chans, width), jnp.float32),
        in_specs=vmem_specs(4),
        out_specs=pl.BlockSpec(memory_space=pltpu.VMEM),
        scratch_shapes=[
            pltpu.VMEM((total, 27 * filters), jnp.bfloat16),
            pltpu.VMEM((depth + 2, height + 2, 3 * filters, width), jnp.bfloat16),
        ],
        compiler_params=pltpu.CompilerParams(vmem_limit_bytes=VMEM_LIMIT),
        cost_estimate=pl.CostEstimate(
            flops=2 * 27 * filters * total * depth * height * width, bytes_accessed=4 << 20, transcendentals=0
        ),
        name="input_grad",
    )(grad, grad_low, grad_high, taps)


def swap(value, axis, bit):
    count = lax.axis_size(axis)
    return lax.ppermute(value, axis, [(i, i ^ (1 << bit)) for i in range(count)])


def message(values, exponent):
    coded = (values * jnp.exp2(14.0 - exponent)).astype(jnp.float16)
    return jnp.concatenate([coded, exponent.astype(jnp.float16)[None]], axis=0)


def opened(received):
    exponent = received[-1].astype(jnp.float32)
    return received[:-1].astype(jnp.float32) * jnp.exp2(exponent - 14.0), exponent


def shard_places(bits):
    edges = len(bits)
    return tuple(
        sum((shard >> bit & 1) << (edges - 1 - step) for step, bit in enumerate(bits))
        for shard in range(1 << edges)
    )


def reduced(values, exponent, bits):
    here = lax.axis_index("space")
    for bit in bits:
        mine = (here >> bit) & 1
        halves = values.reshape((2, values.shape[0] // 2) + values.shape[1:])
        away = lax.dynamic_index_in_dim(halves, 1 - mine, 0, keepdims=False)
        kept = lax.dynamic_index_in_dim(halves, mine, 0, keepdims=False)
        received, bound = opened(swap(message(away, exponent), "space", bit))
        values = kept + received
        exponent = jnp.maximum(exponent, bound) + 1.0
    return message(values, exponent)


def gathered(coded, bits):
    flips = [0]
    for bit in reversed(bits[1:]):
        coded = jnp.concatenate([coded, swap(coded, "space", bit)], axis=0)
        flips = flips + [flip ^ (1 << bit) for flip in flips]
    others = [flip ^ (1 << bits[0]) for flip in flips]
    return [(coded, flips), (swap(coded, "space", bits[0]), others)]


def decoded(coded, count):
    parts = coded.reshape((count, coded.shape[0] // count) + coded.shape[1:]).astype(jnp.float32)
    return parts[:, :-1] * jnp.exp2(parts[:, -1:] - 14.0)


def assemble_kernel(flips, place, *refs):
    parts, out_ref = refs[:-1], refs[-1]
    for index, (part, part_flips) in enumerate(zip(parts, flips)):
        rows, lanes = part.shape[2:]
        side = place[1] if index < len(parts) // 2 else 1 - place[1]
        for at, flip in enumerate(part_flips):
            start = pl.multiple_of((place[2] ^ flip) * rows, rows)
            for half in range(2):

                @pl.when(side == half)
                def _():
                    out_ref[:, pl.ds(start, rows), half * lanes : (half + 1) * lanes] = part[at]


def assembled(place, near, far, filters):
    parts = [decoded(coded, len(flips)) for coded, flips in near + far]
    flips = [flips for _, flips in near + far]
    lanes = parts[0].shape[-1]
    return pl.pallas_call(
        functools.partial(assemble_kernel, flips),
        out_shape=jax.ShapeDtypeStruct((27, filters, 2 * lanes), jnp.float32),
        in_specs=[pl.BlockSpec(memory_space=pltpu.SMEM)] + vmem_specs(len(parts)),
        out_specs=pl.BlockSpec(memory_space=pltpu.VMEM),
        compiler_params=pltpu.CompilerParams(vmem_limit_bytes=VMEM_LIMIT),
        name="assemble",
    )(place, *parts)


def cube_on_device(volume, kernel, cotangent):
    depth, chans, height, width = volume.shape
    filters = cotangent.shape[1]
    count = lax.axis_size("space")
    scale = 1.0 / math.sqrt(depth * count * height * width)
    here = lax.axis_index("chan")
    place = jnp.stack([here & 1, here >> 1, lax.axis_index("space")]).astype(jnp.int32)
    edges = count.bit_length() - 1
    near_bits = tuple(range(edges))
    far_bits = (1, 0) + tuple(range(2, edges))
    forward = [(i, i + 1) for i in range(count - 1)]
    backward = [(i + 1, i) for i in range(count - 1)]

    own = jnp.transpose(volume, (0, 2, 1, 3))
    far_own = swap(own, "chan", 1)
    other = swap(own, "chan", 0)
    grad = jnp.transpose(cotangent, (0, 2, 1, 3))
    low = lax.ppermute(jnp.stack([grad[-1], own[-1]]), "space", forward)
    high = lax.ppermute(jnp.stack([grad[0], own[0]]), "space", backward)
    grad_low, grad_high = low[0], high[0]

    near, near_bound = kernel_grad_part(
        place, own, other, grad, grad_low, grad_high, scale, shard_places(near_bits)
    )
    far_other = swap(far_own, "chan", 0)
    far, far_bound = kernel_grad_part(
        place, far_own, far_other, grad, grad_low, grad_high, scale, shard_places(far_bits)
    )

    rims = jnp.stack([low[1], high[1]])
    rims = pair(rims, swap(rims, "chan", 0), place[0])
    rims = pair(rims, swap(rims, "chan", 1), place[1])

    terms = input_grad_part(grad, grad_low, grad_high, kernel, chans)
    kept = lax.dynamic_index_in_dim(terms, place[0], 1, keepdims=False)
    away = lax.dynamic_index_in_dim(terms, 1 - place[0], 1, keepdims=False)
    terms = kept + swap(away, "chan", 0)
    kept = lax.dynamic_index_in_dim(terms, place[1], 0, keepdims=False)
    away = lax.dynamic_index_in_dim(terms, 1 - place[1], 0, keepdims=False)
    terms = kept + swap(away, "chan", 1)
    input_grad = jnp.transpose(terms.astype(jnp.bfloat16), (0, 2, 1, 3))

    output = output_part(place, own, other, far_own, far_other, rims, kernel)
    output_map = jnp.transpose(output, (0, 2, 1, 3))

    near = gathered(reduced(near, near_bound, near_bits), near_bits)
    far = gathered(reduced(far, far_bound, far_bits), far_bits)
    kernel_grad = assembled(place, near, far, filters)
    return output_map, input_grad, kernel_grad


def pair(own, other, at):
    return jnp.where(at == 0, jnp.concatenate([own, other], 2), jnp.concatenate([other, own], 2))


def with_halo(block, sides, width):
    for axis, dim in sides:
        count = lax.axis_size(axis)
        forward = [(i, i + 1) for i in range(count - 1)]
        backward = [(target, source) for source, target in forward]
        low = lax.ppermute(
            lax.slice_in_dim(block, block.shape[dim] - width, None, axis=dim), axis, forward
        )
        high = lax.ppermute(lax.slice_in_dim(block, 0, width, axis=dim), axis, backward)
        block = jnp.concatenate([low, block, high], axis=dim)
    return block


def plane_stack(piece, height, width, flipped):
    cells = height * width
    padded = jnp.pad(piece, ((0, 0), (0, 0), (width + 1, width + 1)))
    column = lax.broadcasted_iota(jnp.int32, (1, 1, cells), 2) % width
    windows = []
    for row_step in range(3):
        for col_step in range(3):
            row_from = 2 - row_step if flipped else row_step
            col_from = 2 - col_step if flipped else col_step
            offset = width + 1 + (row_from - 1) * width + (col_from - 1)
            shifted = padded[:, :, offset : offset + cells]
            target = column + (col_from - 1)
            inside = ((target >= 0) & (target < width)).astype(piece.dtype)
            windows.append(shifted * inside)
    return jnp.concatenate(windows, axis=1)


def plain_on_device(volume, kernel, cotangent):
    depth, chans_local, height, width = volume.shape
    filters_local = cotangent.shape[1]
    cells = height * width
    scale_factor = 1.0 / math.sqrt(depth * lax.axis_size("space") * height * width)
    volume_flat = volume.reshape(depth, chans_local, cells)
    grad_flat = cotangent.reshape(depth, filters_local, cells)
    columns = lax.all_to_all(kernel, "chan", split_axis=2, concat_axis=1, tiled=True)
    init_output = jnp.zeros((depth, filters_local, cells), jnp.float32)
    init_input = jnp.zeros((depth, chans_local, cells), jnp.float32)
    rims = with_halo(volume_flat, (("space", 0),), 1)
    piece = lax.all_gather(rims, "chan", axis=1, tiled=True)
    output_acc = init_output
    count = piece.shape[1]
    stacked = plane_stack(piece, height, width, False)
    grads = []
    for depth_step in range(3):
        window = stacked[depth_step : depth_step + depth]
        taps = kernel[9 * depth_step : 9 * depth_step + 9]
        weights = jnp.transpose(taps, (1, 0, 2)).reshape(filters_local, 9 * count)
        output_acc = output_acc + jnp.einsum(
            "fj,zjp->zfp", weights, window, preferred_element_type=jnp.float32
        )
        term = jnp.einsum("zfp,zjp->fj", grad_flat, window, preferred_element_type=jnp.float32)
        grads.append(jnp.transpose(term.reshape(filters_local, 9, count), (1, 0, 2)))
    kernel_acc = jnp.concatenate(grads, axis=0)
    output_acc, kernel_acc = (output_acc, kernel_acc)
    grad_ext = with_halo(grad_flat, (("space", 0),), 1)
    total = init_input
    piece = lax.all_gather(grad_ext, "chan", axis=1, tiled=True)
    count = piece.shape[1]
    stacked = plane_stack(piece, height, width, True)
    for depth_step in range(3):
        window = stacked[2 - depth_step : 2 - depth_step + depth]
        taps = columns[9 * depth_step : 9 * depth_step + 9]
        weights = jnp.transpose(taps, (2, 0, 1)).reshape(chans_local, 9 * count)
        total = total + jnp.einsum(
            "kj,zjp->zkp", weights, window, preferred_element_type=jnp.float32
        )
    kernel_grad = lax.psum(kernel_acc, "space") * scale_factor
    output_map = output_acc.astype(jnp.bfloat16).reshape(depth, filters_local, height, width)
    input_grad = total.astype(jnp.bfloat16).reshape(depth, chans_local, height, width)
    return (output_map, input_grad, kernel_grad)

def on_device(volume, kernel, cotangent):
    count, ways = lax.axis_size("space"), lax.axis_size("chan")
    chans, width = volume.shape[1], volume.shape[3]
    filters = cotangent.shape[1]
    cube = ways == 4 and count >= 4 and count & (count - 1) == 0
    if cube and width == 128 and (2 * chans) % 128 == 0 and filters % (8 * count) == 0:
        return cube_on_device(volume, kernel, cotangent)
    return plain_on_device(volume, kernel, cotangent)


def solution(mesh):
    return jax.shard_map(
        on_device,
        mesh=mesh,
        in_specs=(
            P("space", "chan", None, None),
            P(None, "chan", None),
            P("space", "chan", None, None),
        ),
        out_specs=(
            P("space", "chan", None, None),
            P("space", "chan", None, None),
            P(None, "chan", None),
        ),
        check_vma=False,
    )
```

```python
import functools
import math

import jax
import jax.numpy as jnp
from jax import lax
from jax.experimental import pallas as pl
from jax.experimental.pallas import tpu as pltpu
from jax.sharding import PartitionSpec as P

VMEM_LIMIT = 48 * 1024 * 1024
SMALL_COST = pl.CostEstimate(flops=1, bytes_accessed=1, transcendentals=0)


def specs(count):
    return [pl.BlockSpec(memory_space=pltpu.SMEM)] + [pl.BlockSpec(memory_space=pltpu.VMEM)] * count


def shifted(block, step):
    if step:
        width = block.shape[1]
        lane = lax.broadcasted_iota(jnp.int32, block.shape, 1)
        rolled = pltpu.roll(block.astype(jnp.float32), (-step) % width, 1)
        block = jnp.where((lane + step >= 0) & (lane + step < width), rolled, 0.0)
    return block.astype(jnp.bfloat16)


def edge_row(odd, beside, across, low, row):
    if low:
        return jnp.where(odd == 0, across[row], beside[row])
    return jnp.where(odd == 0, beside[row], across[row])


def kernel_grad_kernel(
    scale, order, place, own, other, grad, beside, across, out_ref, left, right
):
    depth, height, chans, width = own.shape
    filters = grad.shape[2]
    cells = height * width
    span = 2 * chans
    odd = place[2] & 1

    for source, at in ((own, place[0]), (other, 1 - place[0])):
        for plane in range(depth):
            for row in range(height):
                lanes = slice(plane * cells + row * width, plane * cells + (row + 1) * width)
                block = source[plane, row]
                for c in range(3):
                    start = pl.multiple_of(c * span + at * chans, chans)
                    right[pl.ds(start, chans), lanes] = shifted(block, c - 1)

    for plane in range(-1, depth + 1):
        for row in range(height):
            if 0 <= plane < depth:
                block = grad[plane, row]
            else:
                block = edge_row(odd, beside, across, plane < 0, row)
            for a in range(3):
                target = plane + a - 1
                if 0 <= target < depth:
                    for b in range(3):
                        at = row + b - 1
                        if 0 <= at < height:
                            rows = slice((3 * a + b) * filters, (3 * a + b + 1) * filters)
                            left[rows, target * cells + at * width : target * cells + (at + 1) * width] = block
    zero = jnp.zeros((filters, width), left.dtype)
    for a in range(3):
        for plane in range(depth):
            last = plane * cells + cells - width
            left[3 * a * filters : (3 * a + 1) * filters, last : last + width] = zero
            left[(3 * a + 2) * filters : (3 * a + 3) * filters, plane * cells : plane * cells + width] = zero

    total = lax.dot_general(
        left[...], right[...], (((1,), (1,)), ((), ())), preferred_element_type=jnp.float32
    )
    total = total * scale
    peak = jnp.maximum(jnp.max(jnp.abs(total)), 1e-30)
    exponent = jnp.ceil(jnp.log2(jnp.full(out_ref.shape[2:], peak, jnp.float32))) + 1.0
    rows = out_ref.shape[2]
    for shard, at in enumerate(order):
        for tap in range(27):
            a, b, c = tap // 9, tap // 3 % 3, tap % 3
            first = (3 * a + b) * filters + shard * rows
            out_ref[at, tap] = total[first : first + rows, c * span : (c + 1) * span]
        out_ref[at, 27] = exponent


def kernel_grad_part(place, own, other, grad, beside, across, scale, order):
    depth, height, chans, width = own.shape
    filters = grad.shape[2]
    cells = depth * height * width
    rows = filters // len(order)
    return pl.pallas_call(
        functools.partial(kernel_grad_kernel, scale, order),
        out_shape=jax.ShapeDtypeStruct((len(order), 28, rows, 2 * chans), jnp.float32),
        in_specs=specs(5),
        out_specs=specs(1)[1],
        scratch_shapes=[
            pltpu.VMEM((9 * filters, cells), jnp.bfloat16),
            pltpu.VMEM((6 * chans, cells), jnp.bfloat16),
        ],
        compiler_params=pltpu.CompilerParams(vmem_limit_bytes=VMEM_LIMIT),
        cost_estimate=SMALL_COST,
        name="kernel_grad",
    )(place, own, other, grad, beside, across)


def output_kernel(place, own, other, far_own, far_other, taps, out_ref, beside_ref, across_ref, weights, stack, acc):
    depth, height, chans, width = own.shape
    filters, total = taps.shape[1], taps.shape[2]
    for tap in range(27):
        a, b, c = tap // 9, tap // 3 % 3, tap % 3
        weights[(3 * a + b) * filters : (3 * a + b + 1) * filters, c * total : (c + 1) * total] = taps[tap]
    core, row_of, odd = place[0], place[1], place[2] & 1
    homes = (
        2 * row_of + core,
        2 * row_of + 1 - core,
        2 * (1 - row_of) + core,
        2 * (1 - row_of) + 1 - core,
    )
    acc[...] = jnp.zeros_like(acc)
    for plane in range(depth):
        for block, home in zip((own, other, far_own, far_other), homes):
            for row in range(height):
                lanes = slice(row * width, (row + 1) * width)
                for c in range(3):
                    start = pl.multiple_of(c * total + home * chans, chans)
                    stack[pl.ds(start, chans), lanes] = shifted(block[plane, row], c - 1)
        for row in range(0, height, 2):
            part = jnp.dot(
                weights[...], stack[:, row * width : (row + 2) * width], preferred_element_type=jnp.float32
            )
            for a in range(3):
                for b in range(3):
                    block = part[(3 * a + b) * filters : (3 * a + b + 1) * filters]
                    for k in range(2):
                        at = row + k - b + 1
                        if 0 <= at < height:
                            acc[plane - a + 2, at] += block[:, k * width : (k + 1) * width]
    out_ref[...] = acc[1 : depth + 1]
    low, high = acc[0], acc[depth + 1]
    beside_ref[...] = jnp.where(odd == 0, high, low)
    across_ref[...] = jnp.where(odd == 0, low, high)


def output_part(place, own, other, far_own, far_other, taps):
    depth, height, chans, width = own.shape
    filters, total = taps.shape[1], taps.shape[2]
    plane = jax.ShapeDtypeStruct((height, filters, width), jnp.float32)
    return pl.pallas_call(
        output_kernel,
        out_shape=[jax.ShapeDtypeStruct((depth, height, filters, width), jnp.float32), plane, plane],
        in_specs=specs(5),
        out_specs=specs(3)[1:],
        scratch_shapes=[
            pltpu.VMEM((9 * filters, 3 * total), jnp.bfloat16),
            pltpu.VMEM((3 * total, height * width), jnp.bfloat16),
            pltpu.VMEM((depth + 2, height, filters, width), jnp.float32),
        ],
        compiler_params=pltpu.CompilerParams(vmem_limit_bytes=VMEM_LIMIT),
        cost_estimate=SMALL_COST,
        name="output_map",
    )(place, own, other, far_own, far_other, taps)


def input_grad_kernel(place, grad, beside, across, taps, out_ref, weights, stack):
    depth, height, filters, width = grad.shape
    total = taps.shape[2]
    chans = out_ref.shape[4]
    span = 3 * filters
    odd = place[2] & 1
    weights[...] = jnp.transpose(taps[...].reshape(27 * filters, total))
    zero = jnp.zeros((span, width), stack.dtype)
    for plane in range(depth + 2):
        stack[plane, 0] = zero
        stack[plane, height + 1] = zero
        for row in range(height):
            if 0 < plane < depth + 1:
                block = grad[plane - 1, row]
            else:
                block = edge_row(odd, beside, across, plane == 0, row)
            for c in range(3):
                stack[plane, row + 1, c * filters : (c + 1) * filters] = shifted(block, 1 - c)
    for plane in range(depth):
        for row in range(0, height, 2):
            halves = []
            for k in range(2):
                pieces = [stack[plane - a + 2, row + k - b + 2] for a in range(3) for b in range(3)]
                halves.append(jnp.concatenate(pieces, axis=0))
            part = jnp.dot(weights[...], jnp.concatenate(halves, axis=1), preferred_element_type=jnp.float32)
            for k in range(2):
                for block in range(total // chans):
                    out_ref[block // 2, block % 2, plane, row + k] = part[
                        block * chans : (block + 1) * chans, k * width : (k + 1) * width
                    ]


def input_grad_part(place, grad, beside, across, taps, chans):
    depth, height, filters, width = grad.shape
    total = taps.shape[2]
    return pl.pallas_call(
        input_grad_kernel,
        out_shape=jax.ShapeDtypeStruct((2, 2, depth, height, chans, width), jnp.float32),
        in_specs=specs(4),
        out_specs=specs(1)[1],
        scratch_shapes=[
            pltpu.VMEM((total, 27 * filters), jnp.bfloat16),
            pltpu.VMEM((depth + 2, height + 2, 3 * filters, width), jnp.bfloat16),
        ],
        compiler_params=pltpu.CompilerParams(vmem_limit_bytes=VMEM_LIMIT),
        cost_estimate=SMALL_COST,
        name="input_grad",
    )(place, grad, beside, across, taps)


def after(value, *others):
    return lax.optimization_barrier((value,) + others)[0]


def swap(value, axis, bit):
    count = lax.axis_size(axis)
    return lax.ppermute(value, axis, [(i, i ^ (1 << bit)) for i in range(count)])


def across_swap(plane):
    count = lax.axis_size("space")
    pairs = [(i, i + 1) for i in range(1, count - 1, 2)]
    return lax.ppermute(plane, "space", pairs + [(j, i) for i, j in pairs])


def is_head(shards):
    return lax.broadcasted_iota(jnp.int32, shards.shape, 1) == shards.shape[1] - 1


def message(shards):
    factor = jnp.where(is_head(shards), 1.0, jnp.exp2(14.0 - shards[:, -1:]))
    return (shards * factor).astype(jnp.float16)


def opened(received):
    shards = received.astype(jnp.float32)
    return shards * jnp.where(is_head(shards), 1.0, jnp.exp2(shards[:, -1:] - 14.0))


def summed(kept, received):
    terms = opened(received)
    return jnp.where(is_head(kept), jnp.maximum(kept, terms) + 1.0, kept + terms)


def cut(shards, bit):
    mine = (lax.axis_index("space") >> bit) & 1
    halves = shards.reshape((2, shards.shape[0] // 2) + shards.shape[1:])
    away = lax.dynamic_index_in_dim(halves, 1 - mine, 0, keepdims=False)
    kept = lax.dynamic_index_in_dim(halves, mine, 0, keepdims=False)
    return kept, message(away)


def shard_places(bits):
    edges = len(bits)
    return tuple(
        sum((shard >> bit & 1) << (edges - 1 - step) for step, bit in enumerate(bits))
        for shard in range(1 << edges)
    )


def assemble_kernel(flips, place, *refs):
    parts, out_ref = refs[:-1], refs[-1]
    for index, (part, part_flips) in enumerate(zip(parts, flips)):
        rows, lanes = part.shape[2:]
        side = place[1] if index < len(parts) // 2 else 1 - place[1]
        for at, flip in enumerate(part_flips):
            start = pl.multiple_of((place[2] ^ flip) * rows, rows)
            for half in range(2):

                @pl.when(side == half)
                def _():
                    out_ref[:, pl.ds(start, rows), half * lanes : (half + 1) * lanes] = part[at, :27]


def assembled(place, parts, flips, filters):
    lanes = parts[0].shape[-1]
    return pl.pallas_call(
        functools.partial(assemble_kernel, flips),
        out_shape=jax.ShapeDtypeStruct((27, filters, 2 * lanes), jnp.float32),
        in_specs=specs(len(parts)),
        out_specs=specs(1)[1],
        compiler_params=pltpu.CompilerParams(vmem_limit_bytes=VMEM_LIMIT),
        cost_estimate=SMALL_COST,
        name="assemble",
    )(place, *parts)


def cube_on_device(volume, kernel, cotangent):
    depth, chans, height, width = volume.shape
    filters = cotangent.shape[1]
    count = lax.axis_size("space")
    scale = 1.0 / math.sqrt(depth * count * height * width)
    here = lax.axis_index("chan")
    place = jnp.stack([here & 1, here >> 1, lax.axis_index("space")]).astype(jnp.int32)
    edges = count.bit_length() - 1
    near_bits = tuple(range(edges))
    far_bits = (1, 0) + tuple(range(2, edges))

    own = jnp.transpose(volume, (0, 2, 1, 3))
    grad = jnp.transpose(cotangent, (0, 2, 1, 3))
    odd = lax.axis_index("space") & 1
    grad_beside = swap(
        lax.dynamic_index_in_dim(grad, (1 - odd) * (depth - 1), 0, keepdims=False), "space", 0
    )
    grad_across = across_swap(
        lax.dynamic_index_in_dim(grad, odd * (depth - 1), 0, keepdims=False)
    )
    far_own = swap(own, "chan", 1)
    other = swap(own, "chan", 0)
    far_other = swap(after(far_own, grad_beside, grad_across), "chan", 0)
    near = kernel_grad_part(
        place, own, other, grad, grad_beside, grad_across, scale, shard_places(near_bits)
    )
    far = kernel_grad_part(
        place, after(far_own, near), far_other, grad, grad_beside, grad_across, scale, shard_places(far_bits)
    )
    chains = [Chain(after(near, far), near_bits), Chain(far, far_bits)]
    last = after(chains[0].sent, chains[1].sent)

    terms = input_grad_part(place, after(grad, last), grad_beside, grad_across, kernel, chans)
    kept = lax.dynamic_index_in_dim(terms, place[0], 1, keepdims=False)
    away = lax.dynamic_index_in_dim(terms, 1 - place[0], 1, keepdims=False)
    received_terms = swap(away, "chan", 0)

    due = {2: [away]}
    for turn in range(2, 4 * edges):
        chain = chains[turn % 2]
        chain.step([last] + due.get(turn, []))
        last = chain.sent
        if turn == 3:
            half_terms = kept + after(received_terms, last)
            kept = lax.dynamic_index_in_dim(half_terms, place[1], 0, keepdims=False)
            away = lax.dynamic_index_in_dim(half_terms, 1 - place[1], 0, keepdims=False)
            received_terms = swap(away, "chan", 1)
            due[turn + 1] = [away]
        if turn == 5:
            inner, beside, across = output_part(place, after(own, last), other, far_own, far_other, kernel)
            beside, across = swap(beside, "space", 0), across_swap(across)
            due[turn + 1] = [inner]
        if turn == 2 * edges + 1:
            total = kept + after(received_terms, last)
            input_grad = jnp.transpose(total.astype(jnp.bfloat16), (0, 2, 1, 3))
            due[turn + 1] = [input_grad]
        if turn == 2 * edges + 3:
            beside, across = after(beside, last), after(across, last)
            rims = [jnp.where(odd == 0, across, beside), jnp.where(odd == 0, beside, across)]
            rims = jnp.stack(rims[:1] + [jnp.zeros_like(beside)] * (depth - 2) + rims[1:])
            output_map = jnp.transpose((inner + rims).astype(jnp.bfloat16), (0, 2, 1, 3))
            due[turn + 2] = [output_map]
    parts, flips = [], []
    for chain in chains:
        parts += [opened(chain.sent), opened(chain.received)]
        flips += [chain.whose, [flip ^ (1 << chain.bits[0]) for flip in chain.whose]]
    kernel_grad = assembled(place, parts, flips, filters)
    return output_map, input_grad, kernel_grad


class Chain:
    def __init__(self, shards, bits):
        self.bits, self.at, self.whose = bits, 0, [0]
        self.kept, self.sent = cut(shards, bits[0])
        self.received = swap(self.sent, "space", bits[0])

    def step(self, earlier):
        received = after(self.received, *earlier)
        self.at += 1
        edges = len(self.bits)
        if self.at <= edges:
            shards = summed(self.kept, received)
            if self.at < edges:
                bit = self.bits[self.at]
                self.kept, self.sent = cut(shards, bit)
            else:
                bit = self.bits[-1]
                self.sent = message(shards)
        else:
            bit = self.bits[2 * edges - 1 - self.at]
            self.sent = jnp.concatenate([self.sent, received], axis=0)
            flip = 1 << self.bits[2 * edges - self.at]
            self.whose = self.whose + [whose ^ flip for whose in self.whose]
        self.received = swap(self.sent, "space", bit)


def with_halo(block, sides, width):
    for axis, dim in sides:
        count = lax.axis_size(axis)
        forward = [(i, i + 1) for i in range(count - 1)]
        backward = [(target, source) for source, target in forward]
        low = lax.ppermute(
            lax.slice_in_dim(block, block.shape[dim] - width, None, axis=dim), axis, forward
        )
        high = lax.ppermute(lax.slice_in_dim(block, 0, width, axis=dim), axis, backward)
        block = jnp.concatenate([low, block, high], axis=dim)
    return block


def plane_stack(piece, height, width, flipped):
    cells = height * width
    padded = jnp.pad(piece, ((0, 0), (0, 0), (width + 1, width + 1)))
    column = lax.broadcasted_iota(jnp.int32, (1, 1, cells), 2) % width
    windows = []
    for row_step in range(3):
        for col_step in range(3):
            row_from = 2 - row_step if flipped else row_step
            col_from = 2 - col_step if flipped else col_step
            offset = width + 1 + (row_from - 1) * width + (col_from - 1)
            shifted = padded[:, :, offset : offset + cells]
            target = column + (col_from - 1)
            inside = ((target >= 0) & (target < width)).astype(piece.dtype)
            windows.append(shifted * inside)
    return jnp.concatenate(windows, axis=1)


def plain_on_device(volume, kernel, cotangent):
    depth, chans_local, height, width = volume.shape
    filters_local = cotangent.shape[1]
    cells = height * width
    scale_factor = 1.0 / math.sqrt(depth * lax.axis_size("space") * height * width)
    volume_flat = volume.reshape(depth, chans_local, cells)
    grad_flat = cotangent.reshape(depth, filters_local, cells)
    columns = lax.all_to_all(kernel, "chan", split_axis=2, concat_axis=1, tiled=True)
    init_output = jnp.zeros((depth, filters_local, cells), jnp.float32)
    init_input = jnp.zeros((depth, chans_local, cells), jnp.float32)
    rims = with_halo(volume_flat, (("space", 0),), 1)
    piece = lax.all_gather(rims, "chan", axis=1, tiled=True)
    output_acc = init_output
    count = piece.shape[1]
    stacked = plane_stack(piece, height, width, False)
    grads = []
    for depth_step in range(3):
        window = stacked[depth_step : depth_step + depth]
        taps = kernel[9 * depth_step : 9 * depth_step + 9]
        weights = jnp.transpose(taps, (1, 0, 2)).reshape(filters_local, 9 * count)
        output_acc = output_acc + jnp.einsum(
            "fj,zjp->zfp", weights, window, preferred_element_type=jnp.float32
        )
        term = jnp.einsum("zfp,zjp->fj", grad_flat, window, preferred_element_type=jnp.float32)
        grads.append(jnp.transpose(term.reshape(filters_local, 9, count), (1, 0, 2)))
    kernel_acc = jnp.concatenate(grads, axis=0)
    output_acc, kernel_acc = (output_acc, kernel_acc)
    grad_ext = with_halo(grad_flat, (("space", 0),), 1)
    total = init_input
    piece = lax.all_gather(grad_ext, "chan", axis=1, tiled=True)
    count = piece.shape[1]
    stacked = plane_stack(piece, height, width, True)
    for depth_step in range(3):
        window = stacked[2 - depth_step : 2 - depth_step + depth]
        taps = columns[9 * depth_step : 9 * depth_step + 9]
        weights = jnp.transpose(taps, (2, 0, 1)).reshape(chans_local, 9 * count)
        total = total + jnp.einsum(
            "kj,zjp->zkp", weights, window, preferred_element_type=jnp.float32
        )
    kernel_grad = lax.psum(kernel_acc, "space") * scale_factor
    output_map = output_acc.astype(jnp.bfloat16).reshape(depth, filters_local, height, width)
    input_grad = total.astype(jnp.bfloat16).reshape(depth, chans_local, height, width)
    return (output_map, input_grad, kernel_grad)

def on_device(volume, kernel, cotangent):
    count, ways = lax.axis_size("space"), lax.axis_size("chan")
    chans, width = volume.shape[1], volume.shape[3]
    filters = cotangent.shape[1]
    cube = ways == 4 and count >= 4 and count & (count - 1) == 0 and volume.shape[0] >= 2
    if cube and width == 128 and (2 * chans) % 128 == 0 and filters % (8 * count) == 0:
        return cube_on_device(volume, kernel, cotangent)
    return plain_on_device(volume, kernel, cotangent)


def solution(mesh):
    return jax.shard_map(
        on_device,
        mesh=mesh,
        in_specs=(
            P("space", "chan", None, None),
            P(None, "chan", None),
            P("space", "chan", None, None),
        ),
        out_specs=(
            P("space", "chan", None, None),
            P("space", "chan", None, None),
            P(None, "chan", None),
        ),
        check_vma=False,
    )
```

```python
import functools
import math

import jax
import jax.numpy as jnp
from jax import lax
from jax.experimental import pallas as pl
from jax.experimental.pallas import tpu as pltpu
from jax.sharding import PartitionSpec as P

VMEM_LIMIT = 48 * 1024 * 1024
SMALL_COST = pl.CostEstimate(flops=1, bytes_accessed=1, transcendentals=0)


def specs(count):
    return [pl.BlockSpec(memory_space=pltpu.SMEM)] + [pl.BlockSpec(memory_space=pltpu.VMEM)] * count


def shifted(block, step):
    if step:
        width = block.shape[1]
        lane = lax.broadcasted_iota(jnp.int32, block.shape, 1)
        rolled = pltpu.roll(block.astype(jnp.float32), (-step) % width, 1)
        block = jnp.where((lane + step >= 0) & (lane + step < width), rolled, 0.0)
    return block.astype(jnp.bfloat16)


def edge_row(odd, beside, across, low, row):
    if low:
        return jnp.where(odd == 0, across[row], beside[row])
    return jnp.where(odd == 0, beside[row], across[row])


def kernel_grad_kernel(
    scale, order, place, own, other, grad, beside, across, out_ref, left, right
):
    depth, height, chans, width = own.shape
    filters = grad.shape[2]
    cells = height * width
    span = 2 * chans
    odd = place[2] & 1

    for source, at in ((own, place[0]), (other, 1 - place[0])):
        for plane in range(depth):
            for row in range(height):
                lanes = slice(plane * cells + row * width, plane * cells + (row + 1) * width)
                block = source[plane, row]
                for c in range(3):
                    start = pl.multiple_of(c * span + at * chans, chans)
                    right[pl.ds(start, chans), lanes] = shifted(block, c - 1)

    for plane in range(-1, depth + 1):
        for row in range(height):
            if 0 <= plane < depth:
                block = grad[plane, row]
            else:
                block = edge_row(odd, beside, across, plane < 0, row)
            for a in range(3):
                target = plane + a - 1
                if 0 <= target < depth:
                    for b in range(3):
                        at = row + b - 1
                        if 0 <= at < height:
                            rows = slice((3 * a + b) * filters, (3 * a + b + 1) * filters)
                            left[rows, target * cells + at * width : target * cells + (at + 1) * width] = block
    zero = jnp.zeros((filters, width), left.dtype)
    for a in range(3):
        for plane in range(depth):
            last = plane * cells + cells - width
            left[3 * a * filters : (3 * a + 1) * filters, last : last + width] = zero
            left[(3 * a + 2) * filters : (3 * a + 3) * filters, plane * cells : plane * cells + width] = zero

    total = lax.dot_general(
        left[...], right[...], (((1,), (1,)), ((), ())), preferred_element_type=jnp.float32
    )
    total = total * scale
    peak = jnp.maximum(jnp.max(jnp.abs(total)), 1e-30)
    exponent = jnp.ceil(jnp.log2(jnp.full(out_ref.shape[2:], peak, jnp.float32))) + 1.0
    rows = out_ref.shape[2]
    for shard, at in enumerate(order):
        for tap in range(27):
            a, b, c = tap // 9, tap // 3 % 3, tap % 3
            first = (3 * a + b) * filters + shard * rows
            out_ref[at, tap] = total[first : first + rows, c * span : (c + 1) * span]
        out_ref[at, 27] = exponent


def kernel_grad_part(place, own, other, grad, beside, across, scale, order):
    depth, height, chans, width = own.shape
    filters = grad.shape[2]
    cells = depth * height * width
    rows = filters // len(order)
    return pl.pallas_call(
        functools.partial(kernel_grad_kernel, scale, order),
        out_shape=jax.ShapeDtypeStruct((len(order), 28, rows, 2 * chans), jnp.float32),
        in_specs=specs(5),
        out_specs=specs(1)[1],
        scratch_shapes=[
            pltpu.VMEM((9 * filters, cells), jnp.bfloat16),
            pltpu.VMEM((6 * chans, cells), jnp.bfloat16),
        ],
        compiler_params=pltpu.CompilerParams(vmem_limit_bytes=VMEM_LIMIT),
        cost_estimate=SMALL_COST,
        name="kernel_grad",
    )(place, own, other, grad, beside, across)


def output_kernel(place, own, other, far_own, far_other, taps, out_ref, beside_ref, across_ref, weights, stack, acc):
    depth, height, chans, width = own.shape
    filters, total = taps.shape[1], taps.shape[2]
    for tap in range(27):
        a, b, c = tap // 9, tap // 3 % 3, tap % 3
        weights[(3 * a + b) * filters : (3 * a + b + 1) * filters, c * total : (c + 1) * total] = taps[tap]
    core, row_of, odd = place[0], place[1], place[2] & 1
    homes = (
        2 * row_of + core,
        2 * row_of + 1 - core,
        2 * (1 - row_of) + core,
        2 * (1 - row_of) + 1 - core,
    )
    acc[...] = jnp.zeros_like(acc)
    for plane in range(depth):
        for block, home in zip((own, other, far_own, far_other), homes):
            for row in range(height):
                lanes = slice(row * width, (row + 1) * width)
                for c in range(3):
                    start = pl.multiple_of(c * total + home * chans, chans)
                    stack[pl.ds(start, chans), lanes] = shifted(block[plane, row], c - 1)
        for row in range(0, height, 2):
            part = jnp.dot(
                weights[...], stack[:, row * width : (row + 2) * width], preferred_element_type=jnp.float32
            )
            for a in range(3):
                for b in range(3):
                    block = part[(3 * a + b) * filters : (3 * a + b + 1) * filters]
                    for k in range(2):
                        at = row + k - b + 1
                        if 0 <= at < height:
                            acc[plane - a + 2, at] += block[:, k * width : (k + 1) * width]
    out_ref[...] = acc[1 : depth + 1]
    low, high = acc[0], acc[depth + 1]
    beside_ref[...] = jnp.where(odd == 0, high, low)
    across_ref[...] = jnp.where(odd == 0, low, high)


def output_part(place, own, other, far_own, far_other, taps):
    depth, height, chans, width = own.shape
    filters, total = taps.shape[1], taps.shape[2]
    plane = jax.ShapeDtypeStruct((height, filters, width), jnp.float32)
    return pl.pallas_call(
        output_kernel,
        out_shape=[jax.ShapeDtypeStruct((depth, height, filters, width), jnp.float32), plane, plane],
        in_specs=specs(5),
        out_specs=specs(3)[1:],
        scratch_shapes=[
            pltpu.VMEM((9 * filters, 3 * total), jnp.bfloat16),
            pltpu.VMEM((3 * total, height * width), jnp.bfloat16),
            pltpu.VMEM((depth + 2, height, filters, width), jnp.float32),
        ],
        compiler_params=pltpu.CompilerParams(vmem_limit_bytes=VMEM_LIMIT),
        cost_estimate=SMALL_COST,
        name="output_map",
    )(place, own, other, far_own, far_other, taps)


def input_grad_kernel(place, grad, beside, across, taps, out_ref, weights, stack):
    depth, height, filters, width = grad.shape
    total = taps.shape[2]
    chans = out_ref.shape[4]
    span = 3 * filters
    odd = place[2] & 1
    weights[...] = jnp.transpose(taps[...].reshape(27 * filters, total))
    zero = jnp.zeros((span, width), stack.dtype)
    for plane in range(depth + 2):
        stack[plane, 0] = zero
        stack[plane, height + 1] = zero
        for row in range(height):
            if 0 < plane < depth + 1:
                block = grad[plane - 1, row]
            else:
                block = edge_row(odd, beside, across, plane == 0, row)
            for c in range(3):
                stack[plane, row + 1, c * filters : (c + 1) * filters] = shifted(block, 1 - c)
    for plane in range(depth):
        for row in range(0, height, 2):
            halves = []
            for k in range(2):
                pieces = [stack[plane - a + 2, row + k - b + 2] for a in range(3) for b in range(3)]
                halves.append(jnp.concatenate(pieces, axis=0))
            part = jnp.dot(weights[...], jnp.concatenate(halves, axis=1), preferred_element_type=jnp.float32)
            for k in range(2):
                for block in range(total // chans):
                    out_ref[block % 2, block // 2, plane, row + k] = part[
                        block * chans : (block + 1) * chans, k * width : (k + 1) * width
                    ]


def input_grad_part(place, grad, beside, across, taps, chans):
    depth, height, filters, width = grad.shape
    total = taps.shape[2]
    return pl.pallas_call(
        input_grad_kernel,
        out_shape=jax.ShapeDtypeStruct((2, 2, depth, height, chans, width), jnp.float32),
        in_specs=specs(4),
        out_specs=specs(1)[1],
        scratch_shapes=[
            pltpu.VMEM((total, 27 * filters), jnp.bfloat16),
            pltpu.VMEM((depth + 2, height + 2, 3 * filters, width), jnp.bfloat16),
        ],
        compiler_params=pltpu.CompilerParams(vmem_limit_bytes=VMEM_LIMIT),
        cost_estimate=SMALL_COST,
        name="input_grad",
    )(place, grad, beside, across, taps)


def entry(values, at):
    return lax.dynamic_index_in_dim(values, at, 0, keepdims=False)


def after(value, *others):
    return lax.optimization_barrier((value,) + others)[0]


def swap(value, axis, bit):
    count = lax.axis_size(axis)
    return lax.ppermute(value, axis, [(i, i ^ (1 << bit)) for i in range(count)])


def across_swap(plane):
    count = lax.axis_size("space")
    pairs = [(i, i + 1) for i in range(1, count - 1, 2)]
    return lax.ppermute(plane, "space", pairs + [(j, i) for i, j in pairs])


def is_head(shards):
    return lax.broadcasted_iota(jnp.int32, shards.shape, 1) == shards.shape[1] - 1


def message(shards):
    factor = jnp.where(is_head(shards), 1.0, jnp.exp2(14.0 - shards[:, -1:]))
    return (shards * factor).astype(jnp.float16)


def opened(received):
    shards = received.astype(jnp.float32)
    return shards * jnp.where(is_head(shards), 1.0, jnp.exp2(shards[:, -1:] - 14.0))


def summed(kept, received):
    terms = opened(received)
    return jnp.where(is_head(kept), jnp.maximum(kept, terms) + 1.0, kept + terms)


def cut(shards, bit):
    mine = (lax.axis_index("space") >> bit) & 1
    halves = shards.reshape((2, shards.shape[0] // 2) + shards.shape[1:])
    away = lax.dynamic_index_in_dim(halves, 1 - mine, 0, keepdims=False)
    kept = lax.dynamic_index_in_dim(halves, mine, 0, keepdims=False)
    return kept, message(away)


def shard_places(bits):
    edges = len(bits)
    return tuple(
        sum((shard >> bit & 1) << (edges - 1 - step) for step, bit in enumerate(bits))
        for shard in range(1 << edges)
    )


def assemble_kernel(flips, place, *refs):
    parts, out_ref = refs[:-1], refs[-1]
    for index, (part, part_flips) in enumerate(zip(parts, flips)):
        rows, lanes = part.shape[2:]
        side = place[1] if index < len(parts) // 2 else 1 - place[1]
        for at, flip in enumerate(part_flips):
            start = pl.multiple_of((place[2] ^ flip) * rows, rows)
            for half in range(2):

                @pl.when(side == half)
                def _():
                    out_ref[:, pl.ds(start, rows), half * lanes : (half + 1) * lanes] = part[at, :27]


def assembled(place, parts, flips, filters):
    lanes = parts[0].shape[-1]
    return pl.pallas_call(
        functools.partial(assemble_kernel, flips),
        out_shape=jax.ShapeDtypeStruct((27, filters, 2 * lanes), jnp.float32),
        in_specs=specs(len(parts)),
        out_specs=specs(1)[1],
        compiler_params=pltpu.CompilerParams(vmem_limit_bytes=VMEM_LIMIT),
        cost_estimate=SMALL_COST,
        name="assemble",
    )(place, *parts)


def cube_on_device(volume, kernel, cotangent):
    depth, chans, height, width = volume.shape
    filters = cotangent.shape[1]
    count = lax.axis_size("space")
    scale = 1.0 / math.sqrt(depth * count * height * width)
    here = lax.axis_index("chan")
    place = jnp.stack([here & 1, here >> 1, lax.axis_index("space")]).astype(jnp.int32)
    edges = count.bit_length() - 1
    near_bits = tuple(range(edges))
    far_bits = (1, 0) + tuple(range(2, edges))

    own = jnp.transpose(volume, (0, 2, 1, 3))
    grad = jnp.transpose(cotangent, (0, 2, 1, 3))
    odd = lax.axis_index("space") & 1
    grad_beside = swap(
        lax.dynamic_index_in_dim(grad, (1 - odd) * (depth - 1), 0, keepdims=False), "space", 0
    )
    grad_across = across_swap(
        lax.dynamic_index_in_dim(grad, odd * (depth - 1), 0, keepdims=False)
    )
    far_own = swap(own, "chan", 1)
    other = swap(own, "chan", 0)
    far_other = swap(after(far_own, grad_beside, grad_across), "chan", 0)
    near = kernel_grad_part(
        place, own, other, grad, grad_beside, grad_across, scale, shard_places(near_bits)
    )
    chains = [Chain(near, near_bits)]
    far = kernel_grad_part(
        place, after(far_own, chains[0].sent), far_other, grad, grad_beside, grad_across, scale,
        shard_places(far_bits),
    )
    chains.append(Chain(far, far_bits))
    last = chains[1].sent

    due = {}
    for turn in range(1, 4 * edges):
        if turn > 1:
            chain = chains[turn % 2]
            chain.step([last] + due.get(turn, []))
            last = chain.sent
        if turn == 1:
            terms = input_grad_part(place, after(grad, last), grad_beside, grad_across, kernel, chans)
            kept, away = entry(terms, place[0]), entry(terms, 1 - place[0])
            received_terms = swap(away, "chan", 0)
            due.setdefault(turn + 1, []).append(away)
        if turn == 3:
            terms = kept + after(received_terms, last)
            kept, away = entry(terms, place[1]), entry(terms, 1 - place[1])
            received_terms = swap(away, "chan", 1)
            due.setdefault(turn + 1, []).append(away)
        if turn == 5:
            inner, beside, across = output_part(place, after(own, last), other, far_own, far_other, kernel)
            due.setdefault(turn + 1, []).append(inner)
        if turn == 7:
            beside, across = swap(after(beside, last), "space", 0), across_swap(after(across, last))
        if turn == 7:
            total = kept + after(received_terms, last)
            input_grad = jnp.transpose(total.astype(jnp.bfloat16), (0, 2, 1, 3))
            due.setdefault(turn + 1, []).append(input_grad)
        if turn == 10:
            beside, across = after(beside, last), after(across, last)
            rims = [jnp.where(odd == 0, across, beside), jnp.where(odd == 0, beside, across)]
            rims = jnp.stack(rims[:1] + [jnp.zeros_like(beside)] * (depth - 2) + rims[1:])
            output_map = jnp.transpose((inner + rims).astype(jnp.bfloat16), (0, 2, 1, 3))
            due.setdefault(turn + 2, []).append(output_map)
    parts, flips = [], []
    for chain in chains:
        parts += [opened(chain.sent), opened(chain.received)]
        flips += [chain.whose, [flip ^ (1 << chain.bits[0]) for flip in chain.whose]]
    kernel_grad = assembled(place, parts, flips, filters)
    return output_map, input_grad, kernel_grad


class Chain:
    def __init__(self, shards, bits):
        self.bits, self.at, self.whose = bits, 0, [0]
        self.kept, self.sent = cut(shards, bits[0])
        self.received = swap(self.sent, "space", bits[0])

    def step(self, earlier):
        received = after(self.received, *earlier)
        self.at += 1
        edges = len(self.bits)
        if self.at <= edges:
            shards = summed(self.kept, received)
            if self.at < edges:
                bit = self.bits[self.at]
                self.kept, self.sent = cut(shards, bit)
            else:
                bit = self.bits[-1]
                self.sent = message(shards)
        else:
            bit = self.bits[2 * edges - 1 - self.at]
            self.sent = jnp.concatenate([self.sent, received], axis=0)
            flip = 1 << self.bits[2 * edges - self.at]
            self.whose = self.whose + [whose ^ flip for whose in self.whose]
        self.received = swap(self.sent, "space", bit)


def with_halo(block, sides, width):
    for axis, dim in sides:
        count = lax.axis_size(axis)
        forward = [(i, i + 1) for i in range(count - 1)]
        backward = [(target, source) for source, target in forward]
        low = lax.ppermute(
            lax.slice_in_dim(block, block.shape[dim] - width, None, axis=dim), axis, forward
        )
        high = lax.ppermute(lax.slice_in_dim(block, 0, width, axis=dim), axis, backward)
        block = jnp.concatenate([low, block, high], axis=dim)
    return block


def plane_stack(piece, height, width, flipped):
    cells = height * width
    padded = jnp.pad(piece, ((0, 0), (0, 0), (width + 1, width + 1)))
    column = lax.broadcasted_iota(jnp.int32, (1, 1, cells), 2) % width
    windows = []
    for row_step in range(3):
        for col_step in range(3):
            row_from = 2 - row_step if flipped else row_step
            col_from = 2 - col_step if flipped else col_step
            offset = width + 1 + (row_from - 1) * width + (col_from - 1)
            shifted = padded[:, :, offset : offset + cells]
            target = column + (col_from - 1)
            inside = ((target >= 0) & (target < width)).astype(piece.dtype)
            windows.append(shifted * inside)
    return jnp.concatenate(windows, axis=1)


def plain_on_device(volume, kernel, cotangent):
    depth, chans_local, height, width = volume.shape
    filters_local = cotangent.shape[1]
    cells = height * width
    scale_factor = 1.0 / math.sqrt(depth * lax.axis_size("space") * height * width)
    volume_flat = volume.reshape(depth, chans_local, cells)
    grad_flat = cotangent.reshape(depth, filters_local, cells)
    columns = lax.all_to_all(kernel, "chan", split_axis=2, concat_axis=1, tiled=True)
    init_output = jnp.zeros((depth, filters_local, cells), jnp.float32)
    init_input = jnp.zeros((depth, chans_local, cells), jnp.float32)
    rims = with_halo(volume_flat, (("space", 0),), 1)
    piece = lax.all_gather(rims, "chan", axis=1, tiled=True)
    output_acc = init_output
    count = piece.shape[1]
    stacked = plane_stack(piece, height, width, False)
    grads = []
    for depth_step in range(3):
        window = stacked[depth_step : depth_step + depth]
        taps = kernel[9 * depth_step : 9 * depth_step + 9]
        weights = jnp.transpose(taps, (1, 0, 2)).reshape(filters_local, 9 * count)
        output_acc = output_acc + jnp.einsum(
            "fj,zjp->zfp", weights, window, preferred_element_type=jnp.float32
        )
        term = jnp.einsum("zfp,zjp->fj", grad_flat, window, preferred_element_type=jnp.float32)
        grads.append(jnp.transpose(term.reshape(filters_local, 9, count), (1, 0, 2)))
    kernel_acc = jnp.concatenate(grads, axis=0)
    output_acc, kernel_acc = (output_acc, kernel_acc)
    grad_ext = with_halo(grad_flat, (("space", 0),), 1)
    total = init_input
    piece = lax.all_gather(grad_ext, "chan", axis=1, tiled=True)
    count = piece.shape[1]
    stacked = plane_stack(piece, height, width, True)
    for depth_step in range(3):
        window = stacked[2 - depth_step : 2 - depth_step + depth]
        taps = columns[9 * depth_step : 9 * depth_step + 9]
        weights = jnp.transpose(taps, (2, 0, 1)).reshape(chans_local, 9 * count)
        total = total + jnp.einsum(
            "kj,zjp->zkp", weights, window, preferred_element_type=jnp.float32
        )
    kernel_grad = lax.psum(kernel_acc, "space") * scale_factor
    output_map = output_acc.astype(jnp.bfloat16).reshape(depth, filters_local, height, width)
    input_grad = total.astype(jnp.bfloat16).reshape(depth, chans_local, height, width)
    return (output_map, input_grad, kernel_grad)

def on_device(volume, kernel, cotangent):
    count, ways = lax.axis_size("space"), lax.axis_size("chan")
    chans, width = volume.shape[1], volume.shape[3]
    filters = cotangent.shape[1]
    cube = ways == 4 and count >= 4 and count & (count - 1) == 0 and volume.shape[0] >= 2
    if cube and width == 128 and (2 * chans) % 128 == 0 and filters % (8 * count) == 0:
        return cube_on_device(volume, kernel, cotangent)
    return plain_on_device(volume, kernel, cotangent)


def solution(mesh):
    return jax.shard_map(
        on_device,
        mesh=mesh,
        in_specs=(
            P("space", "chan", None, None),
            P(None, "chan", None),
            P("space", "chan", None, None),
        ),
        out_specs=(
            P("space", "chan", None, None),
            P("space", "chan", None, None),
            P(None, "chan", None),
        ),
        check_vma=False,
    )
```

```python
import functools
import math

import jax
import jax.numpy as jnp
from jax import lax
from jax.experimental import pallas as pl
from jax.experimental.pallas import tpu as pltpu
from jax.sharding import PartitionSpec as P

VMEM_LIMIT = 48 * 1024 * 1024
SMALL_COST = pl.CostEstimate(flops=1, bytes_accessed=1, transcendentals=0)


def specs(count):
    return [pl.BlockSpec(memory_space=pltpu.SMEM)] + [pl.BlockSpec(memory_space=pltpu.VMEM)] * count


def shifted(block, step):
    if step:
        width = block.shape[1]
        lane = lax.broadcasted_iota(jnp.int32, block.shape, 1)
        rolled = pltpu.roll(block.astype(jnp.float32), (-step) % width, 1)
        block = jnp.where((lane + step >= 0) & (lane + step < width), rolled, 0.0)
    return block.astype(jnp.bfloat16)


def edge_row(odd, beside, across, low, row):
    if low:
        return jnp.where(odd == 0, across[row], beside[row])
    return jnp.where(odd == 0, beside[row], across[row])


def kernel_grad_kernel(
    scale, order, place, own, other, grad, beside, across, out_ref, left, right
):
    depth, height, chans, width = own.shape
    filters = grad.shape[2]
    cells = height * width
    span = 2 * chans
    odd = place[2] & 1

    for source, at in ((own, place[0]), (other, 1 - place[0])):
        for plane in range(depth):
            for row in range(height):
                lanes = slice(plane * cells + row * width, plane * cells + (row + 1) * width)
                block = source[plane, row]
                for c in range(3):
                    start = pl.multiple_of(c * span + at * chans, chans)
                    right[pl.ds(start, chans), lanes] = shifted(block, c - 1)

    for plane in range(-1, depth + 1):
        for row in range(height):
            if 0 <= plane < depth:
                block = grad[plane, row]
            else:
                block = edge_row(odd, beside, across, plane < 0, row)
            for a in range(3):
                target = plane + a - 1
                if 0 <= target < depth:
                    for b in range(3):
                        at = row + b - 1
                        if 0 <= at < height:
                            rows = slice((3 * a + b) * filters, (3 * a + b + 1) * filters)
                            left[rows, target * cells + at * width : target * cells + (at + 1) * width] = block
    zero = jnp.zeros((filters, width), left.dtype)
    for a in range(3):
        for plane in range(depth):
            last = plane * cells + cells - width
            left[3 * a * filters : (3 * a + 1) * filters, last : last + width] = zero
            left[(3 * a + 2) * filters : (3 * a + 3) * filters, plane * cells : plane * cells + width] = zero

    total = lax.dot_general(
        left[...], right[...], (((1,), (1,)), ((), ())), preferred_element_type=jnp.float32
    )
    total = total * scale
    peak = jnp.maximum(jnp.max(jnp.abs(total)), 1e-30)
    exponent = jnp.ceil(jnp.log2(jnp.full(out_ref.shape[2:], peak, jnp.float32))) + 1.0
    rows = out_ref.shape[2]
    for shard, at in enumerate(order):
        for tap in range(27):
            a, b, c = tap // 9, tap // 3 % 3, tap % 3
            first = (3 * a + b) * filters + shard * rows
            out_ref[at, tap] = total[first : first + rows, c * span : (c + 1) * span]
        out_ref[at, 27] = exponent


def kernel_grad_part(place, own, other, grad, beside, across, scale, order):
    depth, height, chans, width = own.shape
    filters = grad.shape[2]
    cells = depth * height * width
    rows = filters // len(order)
    return pl.pallas_call(
        functools.partial(kernel_grad_kernel, scale, order),
        out_shape=jax.ShapeDtypeStruct((len(order), 28, rows, 2 * chans), jnp.float32),
        in_specs=specs(5),
        out_specs=specs(1)[1],
        scratch_shapes=[
            pltpu.VMEM((9 * filters, cells), jnp.bfloat16),
            pltpu.VMEM((6 * chans, cells), jnp.bfloat16),
        ],
        compiler_params=pltpu.CompilerParams(vmem_limit_bytes=VMEM_LIMIT),
        cost_estimate=SMALL_COST,
        name="kernel_grad",
    )(place, own, other, grad, beside, across)


def output_kernel(place, own, other, far_own, far_other, taps, out_ref, beside_ref, across_ref, weights, stack, acc):
    depth, height, chans, width = own.shape
    filters, total = taps.shape[1], taps.shape[2]
    for tap in range(27):
        a, b, c = tap // 9, tap // 3 % 3, tap % 3
        weights[(3 * a + b) * filters : (3 * a + b + 1) * filters, c * total : (c + 1) * total] = taps[tap]
    core, row_of, odd = place[0], place[1], place[2] & 1
    homes = (
        2 * row_of + core,
        2 * row_of + 1 - core,
        2 * (1 - row_of) + core,
        2 * (1 - row_of) + 1 - core,
    )
    acc[...] = jnp.zeros_like(acc)
    for plane in range(depth):
        for block, home in zip((own, other, far_own, far_other), homes):
            for row in range(height):
                lanes = slice(row * width, (row + 1) * width)
                for c in range(3):
                    start = pl.multiple_of(c * total + home * chans, chans)
                    stack[pl.ds(start, chans), lanes] = shifted(block[plane, row], c - 1)
        for row in range(0, height, 2):
            part = jnp.dot(
                weights[...], stack[:, row * width : (row + 2) * width], preferred_element_type=jnp.float32
            )
            for a in range(3):
                for b in range(3):
                    block = part[(3 * a + b) * filters : (3 * a + b + 1) * filters]
                    for k in range(2):
                        at = row + k - b + 1
                        if 0 <= at < height:
                            acc[plane - a + 2, at] += block[:, k * width : (k + 1) * width]
    out_ref[...] = acc[1 : depth + 1]
    low, high = acc[0], acc[depth + 1]
    beside_ref[...] = jnp.where(odd == 0, high, low)
    across_ref[...] = jnp.where(odd == 0, low, high)


def output_part(place, own, other, far_own, far_other, taps):
    depth, height, chans, width = own.shape
    filters, total = taps.shape[1], taps.shape[2]
    plane = jax.ShapeDtypeStruct((height, filters, width), jnp.float32)
    return pl.pallas_call(
        output_kernel,
        out_shape=[jax.ShapeDtypeStruct((depth, height, filters, width), jnp.float32), plane, plane],
        in_specs=specs(5),
        out_specs=specs(3)[1:],
        scratch_shapes=[
            pltpu.VMEM((9 * filters, 3 * total), jnp.bfloat16),
            pltpu.VMEM((3 * total, height * width), jnp.bfloat16),
            pltpu.VMEM((depth + 2, height, filters, width), jnp.float32),
        ],
        compiler_params=pltpu.CompilerParams(vmem_limit_bytes=VMEM_LIMIT),
        cost_estimate=SMALL_COST,
        name="output_map",
    )(place, own, other, far_own, far_other, taps)


def input_grad_kernel(place, grad, beside, across, taps, out_ref, weights, stack):
    depth, height, filters, width = grad.shape
    total = taps.shape[2]
    chans = out_ref.shape[4]
    span = 3 * filters
    odd = place[2] & 1
    weights[...] = jnp.transpose(taps[...].reshape(27 * filters, total))
    zero = jnp.zeros((span, width), stack.dtype)
    for plane in range(depth + 2):
        stack[plane, 0] = zero
        stack[plane, height + 1] = zero
        for row in range(height):
            if 0 < plane < depth + 1:
                block = grad[plane - 1, row]
            else:
                block = edge_row(odd, beside, across, plane == 0, row)
            for c in range(3):
                stack[plane, row + 1, c * filters : (c + 1) * filters] = shifted(block, 1 - c)
    for plane in range(depth):
        for row in range(0, height, 2):
            halves = []
            for k in range(2):
                pieces = [stack[plane - a + 2, row + k - b + 2] for a in range(3) for b in range(3)]
                halves.append(jnp.concatenate(pieces, axis=0))
            part = jnp.dot(weights[...], jnp.concatenate(halves, axis=1), preferred_element_type=jnp.float32)
            for k in range(2):
                for block in range(total // chans):
                    out_ref[block % 2, block // 2, plane, row + k] = part[
                        block * chans : (block + 1) * chans, k * width : (k + 1) * width
                    ]


def input_grad_part(place, grad, beside, across, taps, chans):
    depth, height, filters, width = grad.shape
    total = taps.shape[2]
    return pl.pallas_call(
        input_grad_kernel,
        out_shape=jax.ShapeDtypeStruct((2, 2, depth, height, chans, width), jnp.float32),
        in_specs=specs(4),
        out_specs=specs(1)[1],
        scratch_shapes=[
            pltpu.VMEM((total, 27 * filters), jnp.bfloat16),
            pltpu.VMEM((depth + 2, height + 2, 3 * filters, width), jnp.bfloat16),
        ],
        compiler_params=pltpu.CompilerParams(vmem_limit_bytes=VMEM_LIMIT),
        cost_estimate=SMALL_COST,
        name="input_grad",
    )(place, grad, beside, across, taps)


def entry(values, at):
    return lax.dynamic_index_in_dim(values, at, 0, keepdims=False)


def after(value, *others):
    return lax.optimization_barrier((value,) + others)[0]


def swap(value, axis, bit):
    count = lax.axis_size(axis)
    return lax.ppermute(value, axis, [(i, i ^ (1 << bit)) for i in range(count)])


def across_swap(plane):
    count = lax.axis_size("space")
    pairs = [(i, i + 1) for i in range(1, count - 1, 2)]
    return lax.ppermute(plane, "space", pairs + [(j, i) for i, j in pairs])


def is_head(shards):
    return lax.broadcasted_iota(jnp.int32, shards.shape, 1) == shards.shape[1] - 1


def message(shards):
    factor = jnp.where(is_head(shards), 1.0, jnp.exp2(14.0 - shards[:, -1:]))
    return (shards * factor).astype(jnp.float16)


def opened(received):
    shards = received.astype(jnp.float32)
    return shards * jnp.where(is_head(shards), 1.0, jnp.exp2(shards[:, -1:] - 14.0))


def summed(kept, received):
    terms = opened(received)
    return jnp.where(is_head(kept), jnp.maximum(kept, terms) + 1.0, kept + terms)


def cut(shards, bit):
    mine = (lax.axis_index("space") >> bit) & 1
    halves = shards.reshape((2, shards.shape[0] // 2) + shards.shape[1:])
    away = lax.dynamic_index_in_dim(halves, 1 - mine, 0, keepdims=False)
    kept = lax.dynamic_index_in_dim(halves, mine, 0, keepdims=False)
    return kept, message(away)


def shard_places(bits):
    edges = len(bits)
    return tuple(
        sum((shard >> bit & 1) << (edges - 1 - step) for step, bit in enumerate(bits))
        for shard in range(1 << edges)
    )


def assemble_kernel(flips, place, *refs):
    parts, out_ref = refs[:-1], refs[-1]
    for index, (part, part_flips) in enumerate(zip(parts, flips)):
        rows, lanes = part.shape[2:]
        side = place[1] if index < len(parts) // 2 else 1 - place[1]
        for at, flip in enumerate(part_flips):
            start = pl.multiple_of((place[2] ^ flip) * rows, rows)
            for half in range(2):

                @pl.when(side == half)
                def _():
                    out_ref[:, pl.ds(start, rows), half * lanes : (half + 1) * lanes] = part[at, :27]


def assembled(place, parts, flips, filters):
    lanes = parts[0].shape[-1]
    return pl.pallas_call(
        functools.partial(assemble_kernel, flips),
        out_shape=jax.ShapeDtypeStruct((27, filters, 2 * lanes), jnp.float32),
        in_specs=specs(len(parts)),
        out_specs=specs(1)[1],
        compiler_params=pltpu.CompilerParams(vmem_limit_bytes=VMEM_LIMIT),
        cost_estimate=SMALL_COST,
        name="assemble",
    )(place, *parts)


def cube_on_device(volume, kernel, cotangent):
    depth, chans, height, width = volume.shape
    filters = cotangent.shape[1]
    count = lax.axis_size("space")
    scale = 1.0 / math.sqrt(depth * count * height * width)
    here = lax.axis_index("chan")
    place = jnp.stack([here & 1, here >> 1, lax.axis_index("space")]).astype(jnp.int32)
    edges = count.bit_length() - 1
    near_bits = tuple(range(edges))
    far_bits = (1, 0) + tuple(range(2, edges))

    own = jnp.transpose(volume, (0, 2, 1, 3))
    grad = jnp.transpose(cotangent, (0, 2, 1, 3))
    odd = lax.axis_index("space") & 1
    grad_beside = swap(
        lax.dynamic_index_in_dim(grad, (1 - odd) * (depth - 1), 0, keepdims=False), "space", 0
    )
    grad_across = across_swap(
        lax.dynamic_index_in_dim(grad, odd * (depth - 1), 0, keepdims=False)
    )
    far_own = swap(own, "chan", 1)
    other = swap(own, "chan", 0)
    far_other = swap(after(far_own, grad_beside, grad_across), "chan", 0)
    near = kernel_grad_part(
        place, own, other, grad, grad_beside, grad_across, scale, shard_places(near_bits)
    )
    chains = [Chain(near, near_bits)]
    far = kernel_grad_part(
        place, after(far_own, chains[0].sent), far_other, grad, grad_beside, grad_across, scale,
        shard_places(far_bits),
    )
    chains.append(Chain(far, far_bits))
    last = chains[1].sent

    due = {}
    for turn in range(1, 4 * edges):
        if turn > 1:
            chain = chains[turn % 2]
            chain.step([last] + due.get(turn, []))
            last = chain.sent
        if turn == 1:
            terms = input_grad_part(place, after(grad, last), grad_beside, grad_across, kernel, chans)
            kept, away = entry(terms, place[0]), entry(terms, 1 - place[0])
            received_terms = swap(away, "chan", 0)
            due.setdefault(turn + 1, []).append(away)
        if turn == 3:
            terms = kept + after(received_terms, last)
            kept, away = entry(terms, place[1]), entry(terms, 1 - place[1])
            received_terms = swap(away, "chan", 1)
            due.setdefault(turn + 1, []).append(away)
        if turn == 5:
            inner, beside, across = output_part(place, after(own, last), other, far_own, far_other, kernel)
            due.setdefault(turn + 1, []).append(inner)
        if turn == 8:
            beside = swap(after(beside, last), "space", 0)
        if turn == 7:
            across = across_swap(after(across, last))
        if turn == 7:
            total = kept + after(received_terms, last)
            input_grad = jnp.transpose(total.astype(jnp.bfloat16), (0, 2, 1, 3))
            due.setdefault(turn + 1, []).append(input_grad)
        if turn == 10:
            beside, across = after(beside, last), after(across, last)
            rims = [jnp.where(odd == 0, across, beside), jnp.where(odd == 0, beside, across)]
            rims = jnp.stack(rims[:1] + [jnp.zeros_like(beside)] * (depth - 2) + rims[1:])
            output_map = jnp.transpose((inner + rims).astype(jnp.bfloat16), (0, 2, 1, 3))
            due.setdefault(turn + 2, []).append(output_map)
    parts, flips = [], []
    for chain in chains:
        parts += [opened(chain.sent), opened(chain.received)]
        flips += [chain.whose, [flip ^ (1 << chain.bits[0]) for flip in chain.whose]]
    kernel_grad = assembled(place, parts, flips, filters)
    return output_map, input_grad, kernel_grad


class Chain:
    def __init__(self, shards, bits):
        self.bits, self.at, self.whose = bits, 0, [0]
        self.kept, self.sent = cut(shards, bits[0])
        self.received = swap(self.sent, "space", bits[0])

    def step(self, earlier):
        received = after(self.received, *earlier)
        self.at += 1
        edges = len(self.bits)
        if self.at <= edges:
            shards = summed(self.kept, received)
            if self.at < edges:
                bit = self.bits[self.at]
                self.kept, self.sent = cut(shards, bit)
            else:
                bit = self.bits[-1]
                self.sent = message(shards)
        else:
            bit = self.bits[2 * edges - 1 - self.at]
            self.sent = jnp.concatenate([self.sent, received], axis=0)
            flip = 1 << self.bits[2 * edges - self.at]
            self.whose = self.whose + [whose ^ flip for whose in self.whose]
        self.received = swap(self.sent, "space", bit)


def with_halo(block, sides, width):
    for axis, dim in sides:
        count = lax.axis_size(axis)
        forward = [(i, i + 1) for i in range(count - 1)]
        backward = [(target, source) for source, target in forward]
        low = lax.ppermute(
            lax.slice_in_dim(block, block.shape[dim] - width, None, axis=dim), axis, forward
        )
        high = lax.ppermute(lax.slice_in_dim(block, 0, width, axis=dim), axis, backward)
        block = jnp.concatenate([low, block, high], axis=dim)
    return block


def plane_stack(piece, height, width, flipped):
    cells = height * width
    padded = jnp.pad(piece, ((0, 0), (0, 0), (width + 1, width + 1)))
    column = lax.broadcasted_iota(jnp.int32, (1, 1, cells), 2) % width
    windows = []
    for row_step in range(3):
        for col_step in range(3):
            row_from = 2 - row_step if flipped else row_step
            col_from = 2 - col_step if flipped else col_step
            offset = width + 1 + (row_from - 1) * width + (col_from - 1)
            shifted = padded[:, :, offset : offset + cells]
            target = column + (col_from - 1)
            inside = ((target >= 0) & (target < width)).astype(piece.dtype)
            windows.append(shifted * inside)
    return jnp.concatenate(windows, axis=1)


def plain_on_device(volume, kernel, cotangent):
    depth, chans_local, height, width = volume.shape
    filters_local = cotangent.shape[1]
    cells = height * width
    scale_factor = 1.0 / math.sqrt(depth * lax.axis_size("space") * height * width)
    volume_flat = volume.reshape(depth, chans_local, cells)
    grad_flat = cotangent.reshape(depth, filters_local, cells)
    columns = lax.all_to_all(kernel, "chan", split_axis=2, concat_axis=1, tiled=True)
    init_output = jnp.zeros((depth, filters_local, cells), jnp.float32)
    init_input = jnp.zeros((depth, chans_local, cells), jnp.float32)
    rims = with_halo(volume_flat, (("space", 0),), 1)
    piece = lax.all_gather(rims, "chan", axis=1, tiled=True)
    output_acc = init_output
    count = piece.shape[1]
    stacked = plane_stack(piece, height, width, False)
    grads = []
    for depth_step in range(3):
        window = stacked[depth_step : depth_step + depth]
        taps = kernel[9 * depth_step : 9 * depth_step + 9]
        weights = jnp.transpose(taps, (1, 0, 2)).reshape(filters_local, 9 * count)
        output_acc = output_acc + jnp.einsum(
            "fj,zjp->zfp", weights, window, preferred_element_type=jnp.float32
        )
        term = jnp.einsum("zfp,zjp->fj", grad_flat, window, preferred_element_type=jnp.float32)
        grads.append(jnp.transpose(term.reshape(filters_local, 9, count), (1, 0, 2)))
    kernel_acc = jnp.concatenate(grads, axis=0)
    output_acc, kernel_acc = (output_acc, kernel_acc)
    grad_ext = with_halo(grad_flat, (("space", 0),), 1)
    total = init_input
    piece = lax.all_gather(grad_ext, "chan", axis=1, tiled=True)
    count = piece.shape[1]
    stacked = plane_stack(piece, height, width, True)
    for depth_step in range(3):
        window = stacked[2 - depth_step : 2 - depth_step + depth]
        taps = columns[9 * depth_step : 9 * depth_step + 9]
        weights = jnp.transpose(taps, (2, 0, 1)).reshape(chans_local, 9 * count)
        total = total + jnp.einsum(
            "kj,zjp->zkp", weights, window, preferred_element_type=jnp.float32
        )
    kernel_grad = lax.psum(kernel_acc, "space") * scale_factor
    output_map = output_acc.astype(jnp.bfloat16).reshape(depth, filters_local, height, width)
    input_grad = total.astype(jnp.bfloat16).reshape(depth, chans_local, height, width)
    return (output_map, input_grad, kernel_grad)

def on_device(volume, kernel, cotangent):
    count, ways = lax.axis_size("space"), lax.axis_size("chan")
    chans, width = volume.shape[1], volume.shape[3]
    filters = cotangent.shape[1]
    cube = ways == 4 and count >= 4 and count & (count - 1) == 0 and volume.shape[0] >= 2
    if cube and width == 128 and (2 * chans) % 128 == 0 and filters % (8 * count) == 0:
        return cube_on_device(volume, kernel, cotangent)
    return plain_on_device(volume, kernel, cotangent)


def solution(mesh):
    return jax.shard_map(
        on_device,
        mesh=mesh,
        in_specs=(
            P("space", "chan", None, None),
            P(None, "chan", None),
            P("space", "chan", None, None),
        ),
        out_specs=(
            P("space", "chan", None, None),
            P("space", "chan", None, None),
            P(None, "chan", None),
        ),
        check_vma=False,
    )
```

```python
import functools
import math

import jax
import jax.numpy as jnp
from jax import lax
from jax.experimental import pallas as pl
from jax.experimental.pallas import tpu as pltpu
from jax.sharding import PartitionSpec as P

VMEM_LIMIT = 48 * 1024 * 1024
SMALL_COST = pl.CostEstimate(flops=1, bytes_accessed=1, transcendentals=0)


def specs(count):
    return [pl.BlockSpec(memory_space=pltpu.SMEM)] + [pl.BlockSpec(memory_space=pltpu.VMEM)] * count


def shifted(block, step):
    if step:
        width = block.shape[1]
        lane = lax.broadcasted_iota(jnp.int32, block.shape, 1)
        rolled = pltpu.roll(block.astype(jnp.float32), (-step) % width, 1)
        block = jnp.where((lane + step >= 0) & (lane + step < width), rolled, 0.0)
    return block.astype(jnp.bfloat16)


def edge_row(odd, beside, across, low, row):
    if low:
        return jnp.where(odd == 0, across[row], beside[row])
    return jnp.where(odd == 0, beside[row], across[row])


def kernel_grad_kernel(
    scale, order, place, own, other, grad, beside, across, out_ref, left, right
):
    depth, height, chans, width = own.shape
    filters = grad.shape[2]
    cells = height * width
    span = 2 * chans
    odd = place[2] & 1

    for source, at in ((own, place[0]), (other, 1 - place[0])):
        for plane in range(depth):
            for row in range(height):
                lanes = slice(plane * cells + row * width, plane * cells + (row + 1) * width)
                block = source[plane, row]
                for c in range(3):
                    start = pl.multiple_of(c * span + at * chans, chans)
                    right[pl.ds(start, chans), lanes] = shifted(block, c - 1)

    for plane in range(-1, depth + 1):
        for row in range(height):
            if 0 <= plane < depth:
                block = grad[plane, row]
            else:
                block = edge_row(odd, beside, across, plane < 0, row)
            for a in range(3):
                target = plane + a - 1
                if 0 <= target < depth:
                    for b in range(3):
                        at = row + b - 1
                        if 0 <= at < height:
                            rows = slice((3 * a + b) * filters, (3 * a + b + 1) * filters)
                            left[rows, target * cells + at * width : target * cells + (at + 1) * width] = block
    zero = jnp.zeros((filters, width), left.dtype)
    for a in range(3):
        for plane in range(depth):
            last = plane * cells + cells - width
            left[3 * a * filters : (3 * a + 1) * filters, last : last + width] = zero
            left[(3 * a + 2) * filters : (3 * a + 3) * filters, plane * cells : plane * cells + width] = zero

    total = lax.dot_general(
        left[...], right[...], (((1,), (1,)), ((), ())), preferred_element_type=jnp.float32
    )
    total = total * scale
    peak = jnp.maximum(jnp.max(jnp.abs(total)), 1e-30)
    exponent = jnp.ceil(jnp.log2(jnp.full(out_ref.shape[2:], peak, jnp.float32))) + 1.0
    rows = out_ref.shape[2]
    for shard, at in enumerate(order):
        for tap in range(27):
            a, b, c = tap // 9, tap // 3 % 3, tap % 3
            first = (3 * a + b) * filters + shard * rows
            out_ref[at, tap] = total[first : first + rows, c * span : (c + 1) * span]
        out_ref[at, 27] = exponent


def kernel_grad_part(place, own, other, grad, beside, across, scale, order):
    depth, height, chans, width = own.shape
    filters = grad.shape[2]
    cells = depth * height * width
    rows = filters // len(order)
    return pl.pallas_call(
        functools.partial(kernel_grad_kernel, scale, order),
        out_shape=jax.ShapeDtypeStruct((len(order), 28, rows, 2 * chans), jnp.float32),
        in_specs=specs(5),
        out_specs=specs(1)[1],
        scratch_shapes=[
            pltpu.VMEM((9 * filters, cells), jnp.bfloat16),
            pltpu.VMEM((6 * chans, cells), jnp.bfloat16),
        ],
        compiler_params=pltpu.CompilerParams(vmem_limit_bytes=VMEM_LIMIT),
        cost_estimate=SMALL_COST,
        name="kernel_grad",
    )(place, own, other, grad, beside, across)


def output_kernel(place, own, other, far_own, far_other, taps, out_ref, beside_ref, across_ref, weights, stack, acc):
    depth, height, chans, width = own.shape
    filters, total = taps.shape[1], taps.shape[2]
    for tap in range(27):
        a, b, c = tap // 9, tap // 3 % 3, tap % 3
        weights[(3 * a + b) * filters : (3 * a + b + 1) * filters, c * total : (c + 1) * total] = taps[tap]
    core, row_of, odd = place[0], place[1], place[2] & 1
    homes = (
        2 * row_of + core,
        2 * row_of + 1 - core,
        2 * (1 - row_of) + core,
        2 * (1 - row_of) + 1 - core,
    )
    acc[...] = jnp.zeros_like(acc)
    for plane in range(depth):
        for block, home in zip((own, other, far_own, far_other), homes):
            for row in range(height):
                lanes = slice(row * width, (row + 1) * width)
                for c in range(3):
                    start = pl.multiple_of(c * total + home * chans, chans)
                    stack[pl.ds(start, chans), lanes] = shifted(block[plane, row], c - 1)
        for row in range(0, height, 2):
            part = jnp.dot(
                weights[...], stack[:, row * width : (row + 2) * width], preferred_element_type=jnp.float32
            )
            for a in range(3):
                for b in range(3):
                    block = part[(3 * a + b) * filters : (3 * a + b + 1) * filters]
                    for k in range(2):
                        at = row + k - b + 1
                        if 0 <= at < height:
                            acc[plane - a + 2, at] += block[:, k * width : (k + 1) * width]
    out_ref[...] = acc[1 : depth + 1]
    low, high = acc[0], acc[depth + 1]
    beside_ref[...] = jnp.where(odd == 0, high, low)
    across_ref[...] = jnp.where(odd == 0, low, high)


def output_part(place, own, other, far_own, far_other, taps):
    depth, height, chans, width = own.shape
    filters, total = taps.shape[1], taps.shape[2]
    plane = jax.ShapeDtypeStruct((height, filters, width), jnp.float32)
    return pl.pallas_call(
        output_kernel,
        out_shape=[jax.ShapeDtypeStruct((depth, height, filters, width), jnp.float32), plane, plane],
        in_specs=specs(5),
        out_specs=specs(3)[1:],
        scratch_shapes=[
            pltpu.VMEM((9 * filters, 3 * total), jnp.bfloat16),
            pltpu.VMEM((3 * total, height * width), jnp.bfloat16),
            pltpu.VMEM((depth + 2, height, filters, width), jnp.float32),
        ],
        compiler_params=pltpu.CompilerParams(vmem_limit_bytes=VMEM_LIMIT),
        cost_estimate=SMALL_COST,
        name="output_map",
    )(place, own, other, far_own, far_other, taps)


def input_grad_kernel(place, grad, beside, across, taps, out_ref, weights, stack):
    depth, height, filters, width = grad.shape
    total = taps.shape[2]
    chans = out_ref.shape[4]
    span = 3 * filters
    odd = place[2] & 1
    weights[...] = jnp.transpose(taps[...].reshape(27 * filters, total))
    zero = jnp.zeros((span, width), stack.dtype)
    for plane in range(depth + 2):
        stack[plane, 0] = zero
        stack[plane, height + 1] = zero
        for row in range(height):
            if 0 < plane < depth + 1:
                block = grad[plane - 1, row]
            else:
                block = edge_row(odd, beside, across, plane == 0, row)
            for c in range(3):
                stack[plane, row + 1, c * filters : (c + 1) * filters] = shifted(block, 1 - c)
    for plane in range(depth):
        for row in range(0, height, 2):
            halves = []
            for k in range(2):
                pieces = [stack[plane - a + 2, row + k - b + 2] for a in range(3) for b in range(3)]
                halves.append(jnp.concatenate(pieces, axis=0))
            part = jnp.dot(weights[...], jnp.concatenate(halves, axis=1), preferred_element_type=jnp.float32)
            for k in range(2):
                for block in range(total // chans):
                    out_ref[block % 2, block // 2, plane, row + k] = part[
                        block * chans : (block + 1) * chans, k * width : (k + 1) * width
                    ]


def input_grad_part(place, grad, beside, across, taps, chans):
    depth, height, filters, width = grad.shape
    total = taps.shape[2]
    return pl.pallas_call(
        input_grad_kernel,
        out_shape=jax.ShapeDtypeStruct((2, 2, depth, height, chans, width), jnp.float32),
        in_specs=specs(4),
        out_specs=specs(1)[1],
        scratch_shapes=[
            pltpu.VMEM((total, 27 * filters), jnp.bfloat16),
            pltpu.VMEM((depth + 2, height + 2, 3 * filters, width), jnp.bfloat16),
        ],
        compiler_params=pltpu.CompilerParams(vmem_limit_bytes=VMEM_LIMIT),
        cost_estimate=SMALL_COST,
        name="input_grad",
    )(place, grad, beside, across, taps)


def entry(values, at):
    return lax.dynamic_index_in_dim(values, at, 0, keepdims=False)


def after(value, *others):
    return lax.optimization_barrier((value,) + others)[0]


def swap(value, axis, bit):
    count = lax.axis_size(axis)
    return lax.ppermute(value, axis, [(i, i ^ (1 << bit)) for i in range(count)])


def across_swap(plane):
    count = lax.axis_size("space")
    pairs = [(i, i + 1) for i in range(1, count - 1, 2)]
    return lax.ppermute(plane, "space", pairs + [(j, i) for i, j in pairs])


def is_head(shards):
    return lax.broadcasted_iota(jnp.int32, shards.shape, 1) == shards.shape[1] - 1


def message(shards):
    factor = jnp.where(is_head(shards), 1.0, jnp.exp2(14.0 - shards[:, -1:]))
    return (shards * factor).astype(jnp.float16)


def opened(received):
    shards = received.astype(jnp.float32)
    return shards * jnp.where(is_head(shards), 1.0, jnp.exp2(shards[:, -1:] - 14.0))


def summed(kept, received):
    terms = opened(received)
    return jnp.where(is_head(kept), jnp.maximum(kept, terms) + 1.0, kept + terms)


def cut(shards, bit):
    mine = (lax.axis_index("space") >> bit) & 1
    halves = shards.reshape((2, shards.shape[0] // 2) + shards.shape[1:])
    away = lax.dynamic_index_in_dim(halves, 1 - mine, 0, keepdims=False)
    kept = lax.dynamic_index_in_dim(halves, mine, 0, keepdims=False)
    return kept, message(away)


def shard_places(bits):
    edges = len(bits)
    return tuple(
        sum((shard >> bit & 1) << (edges - 1 - step) for step, bit in enumerate(bits))
        for shard in range(1 << edges)
    )


def assemble_kernel(flips, place, *refs):
    parts, out_ref = refs[:-1], refs[-1]
    for index, (part, part_flips) in enumerate(zip(parts, flips)):
        rows, lanes = part.shape[2:]
        side = place[1] if index < len(parts) // 2 else 1 - place[1]
        for at, flip in enumerate(part_flips):
            start = pl.multiple_of((place[2] ^ flip) * rows, rows)
            for half in range(2):

                @pl.when(side == half)
                def _():
                    out_ref[:, pl.ds(start, rows), half * lanes : (half + 1) * lanes] = part[at, :27]


def assembled(place, parts, flips, filters):
    lanes = parts[0].shape[-1]
    return pl.pallas_call(
        functools.partial(assemble_kernel, flips),
        out_shape=jax.ShapeDtypeStruct((27, filters, 2 * lanes), jnp.float32),
        in_specs=specs(len(parts)),
        out_specs=specs(1)[1],
        compiler_params=pltpu.CompilerParams(vmem_limit_bytes=VMEM_LIMIT),
        cost_estimate=SMALL_COST,
        name="assemble",
    )(place, *parts)


def cube_on_device(volume, kernel, cotangent):
    depth, chans, height, width = volume.shape
    filters = cotangent.shape[1]
    count = lax.axis_size("space")
    scale = 1.0 / math.sqrt(depth * count * height * width)
    here = lax.axis_index("chan")
    place = jnp.stack([here & 1, here >> 1, lax.axis_index("space")]).astype(jnp.int32)
    edges = count.bit_length() - 1
    near_bits = tuple(range(edges))
    far_bits = (1, 0) + tuple(range(2, edges))

    own = jnp.transpose(volume, (0, 2, 1, 3))
    grad = jnp.transpose(cotangent, (0, 2, 1, 3))
    odd = lax.axis_index("space") & 1
    grad_beside = swap(
        lax.dynamic_index_in_dim(grad, (1 - odd) * (depth - 1), 0, keepdims=False), "space", 0
    )
    grad_across = across_swap(
        lax.dynamic_index_in_dim(grad, odd * (depth - 1), 0, keepdims=False)
    )
    far_own = swap(own, "chan", 1)
    other = swap(own, "chan", 0)
    far_other = swap(after(far_own, grad_beside, grad_across), "chan", 0)
    near = kernel_grad_part(
        place, own, other, grad, grad_beside, grad_across, scale, shard_places(near_bits)
    )
    chains = [Chain(near, near_bits)]
    far = kernel_grad_part(
        place, after(far_own, chains[0].sent), far_other, grad, grad_beside, grad_across, scale,
        shard_places(far_bits),
    )
    chains.append(Chain(far, far_bits))
    last = chains[1].sent

    due = {}
    for turn in range(1, 4 * edges):
        if turn > 1:
            chain = chains[turn % 2]
            chain.step([last] + due.get(turn, []))
            last = chain.sent
        if turn == 1:
            terms = input_grad_part(place, after(grad, last), grad_beside, grad_across, kernel, chans)
            kept, away = entry(terms, place[0]), entry(terms, 1 - place[0])
            received_terms = swap(away, "chan", 0)
            due.setdefault(turn + 1, []).append(away)
        if turn == 3:
            terms = kept + after(received_terms, last)
            kept, away = entry(terms, place[1]), entry(terms, 1 - place[1])
            received_terms = swap(away, "chan", 1)
            due.setdefault(turn + 1, []).append(away)
        if turn == 5:
            inner, beside, across = output_part(place, after(own, last), other, far_own, far_other, kernel)
            due.setdefault(turn + 2, []).append(inner)
        if turn == 8:
            beside = swap(after(beside, last), "space", 0)
        if turn == 7:
            across = across_swap(after(across, last))
        if turn == 9:
            total = kept + after(received_terms, last)
            input_grad = jnp.transpose(total.astype(jnp.bfloat16), (0, 2, 1, 3))
            due.setdefault(turn + 1, []).append(input_grad)
        if turn == 10:
            beside, across = after(beside, last), after(across, last)
            rims = [jnp.where(odd == 0, across, beside), jnp.where(odd == 0, beside, across)]
            rims = jnp.stack(rims[:1] + [jnp.zeros_like(beside)] * (depth - 2) + rims[1:])
            output_map = jnp.transpose((inner + rims).astype(jnp.bfloat16), (0, 2, 1, 3))
            due.setdefault(turn + 2, []).append(output_map)
    parts, flips = [], []
    for chain in chains:
        parts += [opened(chain.sent), opened(chain.received)]
        flips += [chain.whose, [flip ^ (1 << chain.bits[0]) for flip in chain.whose]]
    kernel_grad = assembled(place, parts, flips, filters)
    return output_map, input_grad, kernel_grad


class Chain:
    def __init__(self, shards, bits):
        self.bits, self.at, self.whose = bits, 0, [0]
        self.kept, self.sent = cut(shards, bits[0])
        self.received = swap(self.sent, "space", bits[0])

    def step(self, earlier):
        received = after(self.received, *earlier)
        self.at += 1
        edges = len(self.bits)
        if self.at <= edges:
            shards = summed(self.kept, received)
            if self.at < edges:
                bit = self.bits[self.at]
                self.kept, self.sent = cut(shards, bit)
            else:
                bit = self.bits[-1]
                self.sent = message(shards)
        else:
            bit = self.bits[2 * edges - 1 - self.at]
            self.sent = jnp.concatenate([self.sent, received], axis=0)
            flip = 1 << self.bits[2 * edges - self.at]
            self.whose = self.whose + [whose ^ flip for whose in self.whose]
        self.received = swap(self.sent, "space", bit)


def with_halo(block, sides, width):
    for axis, dim in sides:
        count = lax.axis_size(axis)
        forward = [(i, i + 1) for i in range(count - 1)]
        backward = [(target, source) for source, target in forward]
        low = lax.ppermute(
            lax.slice_in_dim(block, block.shape[dim] - width, None, axis=dim), axis, forward
        )
        high = lax.ppermute(lax.slice_in_dim(block, 0, width, axis=dim), axis, backward)
        block = jnp.concatenate([low, block, high], axis=dim)
    return block


def plane_stack(piece, height, width, flipped):
    cells = height * width
    padded = jnp.pad(piece, ((0, 0), (0, 0), (width + 1, width + 1)))
    column = lax.broadcasted_iota(jnp.int32, (1, 1, cells), 2) % width
    windows = []
    for row_step in range(3):
        for col_step in range(3):
            row_from = 2 - row_step if flipped else row_step
            col_from = 2 - col_step if flipped else col_step
            offset = width + 1 + (row_from - 1) * width + (col_from - 1)
            shifted = padded[:, :, offset : offset + cells]
            target = column + (col_from - 1)
            inside = ((target >= 0) & (target < width)).astype(piece.dtype)
            windows.append(shifted * inside)
    return jnp.concatenate(windows, axis=1)


def plain_on_device(volume, kernel, cotangent):
    depth, chans_local, height, width = volume.shape
    filters_local = cotangent.shape[1]
    cells = height * width
    scale_factor = 1.0 / math.sqrt(depth * lax.axis_size("space") * height * width)
    volume_flat = volume.reshape(depth, chans_local, cells)
    grad_flat = cotangent.reshape(depth, filters_local, cells)
    columns = lax.all_to_all(kernel, "chan", split_axis=2, concat_axis=1, tiled=True)
    init_output = jnp.zeros((depth, filters_local, cells), jnp.float32)
    init_input = jnp.zeros((depth, chans_local, cells), jnp.float32)
    rims = with_halo(volume_flat, (("space", 0),), 1)
    piece = lax.all_gather(rims, "chan", axis=1, tiled=True)
    output_acc = init_output
    count = piece.shape[1]
    stacked = plane_stack(piece, height, width, False)
    grads = []
    for depth_step in range(3):
        window = stacked[depth_step : depth_step + depth]
        taps = kernel[9 * depth_step : 9 * depth_step + 9]
        weights = jnp.transpose(taps, (1, 0, 2)).reshape(filters_local, 9 * count)
        output_acc = output_acc + jnp.einsum(
            "fj,zjp->zfp", weights, window, preferred_element_type=jnp.float32
        )
        term = jnp.einsum("zfp,zjp->fj", grad_flat, window, preferred_element_type=jnp.float32)
        grads.append(jnp.transpose(term.reshape(filters_local, 9, count), (1, 0, 2)))
    kernel_acc = jnp.concatenate(grads, axis=0)
    output_acc, kernel_acc = (output_acc, kernel_acc)
    grad_ext = with_halo(grad_flat, (("space", 0),), 1)
    total = init_input
    piece = lax.all_gather(grad_ext, "chan", axis=1, tiled=True)
    count = piece.shape[1]
    stacked = plane_stack(piece, height, width, True)
    for depth_step in range(3):
        window = stacked[2 - depth_step : 2 - depth_step + depth]
        taps = columns[9 * depth_step : 9 * depth_step + 9]
        weights = jnp.transpose(taps, (2, 0, 1)).reshape(chans_local, 9 * count)
        total = total + jnp.einsum(
            "kj,zjp->zkp", weights, window, preferred_element_type=jnp.float32
        )
    kernel_grad = lax.psum(kernel_acc, "space") * scale_factor
    output_map = output_acc.astype(jnp.bfloat16).reshape(depth, filters_local, height, width)
    input_grad = total.astype(jnp.bfloat16).reshape(depth, chans_local, height, width)
    return (output_map, input_grad, kernel_grad)

def on_device(volume, kernel, cotangent):
    count, ways = lax.axis_size("space"), lax.axis_size("chan")
    chans, width = volume.shape[1], volume.shape[3]
    filters = cotangent.shape[1]
    cube = ways == 4 and count >= 4 and count & (count - 1) == 0 and volume.shape[0] >= 2
    if cube and width == 128 and (2 * chans) % 128 == 0 and filters % (8 * count) == 0:
        return cube_on_device(volume, kernel, cotangent)
    return plain_on_device(volume, kernel, cotangent)


def solution(mesh):
    return jax.shard_map(
        on_device,
        mesh=mesh,
        in_specs=(
            P("space", "chan", None, None),
            P(None, "chan", None),
            P("space", "chan", None, None),
        ),
        out_specs=(
            P("space", "chan", None, None),
            P("space", "chan", None, None),
            P(None, "chan", None),
        ),
        check_vma=False,
    )
```
